32 devices in a mesh: dp: 8 (over y, x, core), expert: 4 (over z).
Axes of the slice: x: 2, y: 2, z: 4, core: 2. Of those that a mesh axis runs over, the one named last changes fastest.
Arguments:
- tokens: bfloat16 [4096, 2048], P(('dp', 'expert')), may hold values from -6 to 6
- teacher: bfloat16 [4096, 2048], P(('dp', 'expert')), may hold values from -6 to 6
- attn_routes: int32 [4096, 2], P(('dp', 'expert')), may hold values from 0 to 3, all different within a row; in each aligned block of 128 rows (0 to 127, 128 to 255, ...) at most 96 rows name the same one
- mlp_routes: int32 [4096, 2], P(('dp', 'expert')), may hold values from 0 to 3, all different within a row; in each aligned block of 128 rows (0 to 127, 128 to 255, ...) at most 96 rows name the same one
- image_mask: int32 [4096], P(('dp', 'expert')), may hold values from 0 to 1, as said below
- valid: int32 [4096], P(('dp', 'expert')), may hold values from 0 to 1
- master_query: float32 [2048, 8192], P('dp', 'expert'), may hold values from -0.125 to 0.125
- moment_query: float32 [2048, 8192], P('dp', 'expert'), may hold values from -0.01875 to 0.01875
- square_query: float32 [2048, 8192], P('dp', 'expert'), may hold values from 1.953125e-05 to 0.0001953125
- master_project: float32 [8192, 2048], P('expert', 'dp'), may hold values from -0.5 to 0.5
- moment_project: float32 [8192, 2048], P('expert', 'dp'), may hold values from -0.00515625 to 0.00515625
- square_project: float32 [8192, 2048], P('expert', 'dp'), may hold values from 1.4648438e-06 to 1.4648437e-05
- master_gate_up: float32 [2, 2048, 22528], P(None, 'dp', 'expert'), may hold values from -0.125 to 0.125
- moment_gate_up: float32 [2, 2048, 22528], P(None, 'dp', 'expert'), may hold values from -0.0075 to 0.0075
- square_gate_up: float32 [2, 2048, 22528], P(None, 'dp', 'expert'), may hold values from 3.125e-06 to 3.125e-05
- master_down: float32 [22528, 2048], P('expert', 'dp'), may hold values from -0.109375 to 0.109375
- moment_down: float32 [22528, 2048], P('expert', 'dp'), may hold values from -0.0103125 to 0.0103125
- square_down: float32 [22528, 2048], P('expert', 'dp'), may hold values from 5.859375e-06 to 5.859375e-05
- master_key_value: float32 [2048, 4096], P(('dp', 'expert')), may hold values from -0.125 to 0.125
- moment_key_value: float32 [2048, 4096], P(('dp', 'expert')), may hold values from -0.080625 to 0.080625
- square_key_value: float32 [2048, 4096], P(('dp', 'expert')), may hold values from 0.00036621094 to 0.0036621094
- master_router: float32 [2048, 8], P(('dp', 'expert')), may hold values from -0.09375 to 0.09375
- moment_router: float32 [2048, 8], P(('dp', 'expert')), may hold values from -2.25 to 2.25
- square_router: float32 [2048, 8], P(('dp', 'expert')), may hold values from 0.28076172 to 2.8076172
- master_gains: float32 [2, 2048], P(None, ('dp', 'expert')), may hold values from 0.5 to 1.5
- moment_gains: float32 [2, 2048], P(None, ('dp', 'expert')), may hold values from -0.6 to 0.6
- square_gains: float32 [2, 2048], P(None, ('dp', 'expert')), may hold values from 0.02 to 0.2
Outputs:
- output: float32 [4096, 2048], P(('dp', 'expert'))
- loss: float32 [], replicated
- input_grad: float32 [4096, 2048], P(('dp', 'expert'))
- query_grad: float32 [2048, 8192], P('dp', 'expert')
- query_direction: float32 [2048, 8192], P('dp', 'expert')
- query_moment: float32 [2048, 8192], P('dp', 'expert')
- query_square: float32 [2048, 8192], P('dp', 'expert')
- project_grad: float32 [8192, 2048], P('expert', 'dp')
- project_direction: float32 [8192, 2048], P('expert', 'dp')
- project_moment: float32 [8192, 2048], P('expert', 'dp')
- project_square: float32 [8192, 2048], P('expert', 'dp')
- gate_up_grad: float32 [2, 2048, 22528], P(None, 'dp', 'expert')
- gate_up_direction: float32 [2, 2048, 22528], P(None, 'dp', 'expert')
- gate_up_moment: float32 [2, 2048, 22528], P(None, 'dp', 'expert')
- gate_up_square: float32 [2, 2048, 22528], P(None, 'dp', 'expert')
- down_grad: float32 [22528, 2048], P('expert', 'dp')
- down_direction: float32 [22528, 2048], P('expert', 'dp')
- down_moment: float32 [22528, 2048], P('expert', 'dp')
- down_square: float32 [22528, 2048], P('expert', 'dp')
- key_value_grad: float32 [2048, 4096], P(('dp', 'expert'))
- key_value_direction: float32 [2048, 4096], P(('dp', 'expert'))
- key_value_moment: float32 [2048, 4096], P(('dp', 'expert'))
- key_value_square: float32 [2048, 4096], P(('dp', 'expert'))
- router_grad: float32 [2048, 8], P(('dp', 'expert'))
- router_direction: float32 [2048, 8], P(('dp', 'expert'))
- router_moment: float32 [2048, 8], P(('dp', 'expert'))
- router_square: float32 [2048, 8], P(('dp', 'expert'))
- gains_grad: float32 [2, 2048], P(None, ('dp', 'expert'))
- gains_direction: float32 [2, 2048], P(None, ('dp', 'expert'))
- gains_moment: float32 [2, 2048], P(None, ('dp', 'expert'))
- gains_square: float32 [2, 2048], P(None, ('dp', 'expert'))
The draws below stay inside these ranges and needn't reach their ends.
Inputs may be any that keep to these rules, and one draw needn't show every extreme that they name: `attn_routes`: in the rows of one device no expert is named by more than 96 rows; the two entries of a row differ. `mlp_routes`: in the rows of one device no expert is named by more than 96 rows; the two entries of a row differ. `image_mask`: in each sequence of 128 tokens the ones form one run of exactly 32 tokens.
All inputs are finite; a program needn't handle non-finite values.
Results may differ from the reference program's by a relative error of at most 0.022.
Values may be sent and summed in bfloat16 or wider, within the bound.
No kernel may reach another device: no remote copies, remote signals or barrier semaphores. Data moves between devices by JAX's collectives and lax.ppermute only.
A program may use at most 344 MiB of HBM per device.

```python
import math
import jax
import jax.numpy as jnp
import numpy as np
from jax import lax

D = 2048
HEADS = 16
HD = 128
FF = 5632
EXPERTS = 4
TOP = 2
TOK_DEV = 128
IMG = 32
STEP = 10
QW = 2048
CAP = 96
TOKENS = 4096


def draw_image_mask(key, part):
    key = jax.random.fold_in(key, 11)
    seq_total = TOKENS // TOK_DEV
    starts = jax.random.randint(key, (seq_total, 1), 0, TOK_DEV - IMG + 1)
    position = jnp.arange(TOK_DEV, dtype=jnp.int32)[None, :]
    inside = (position >= starts) & (position < starts + IMG)
    return inside.astype(jnp.int32).reshape(TOKENS)


def draw_valid(key, part):
    key = jax.random.fold_in(key, 23)
    rolls = jax.random.randint(key, (TOKENS,), 0, 1000)
    place = jnp.arange(TOKENS, dtype=jnp.int32)
    limit = 250 + 650 * (place // TOK_DEV) // (TOKENS // TOK_DEV)
    return (rolls < limit).astype(jnp.int32)


def block_scale(rng, shape, shards, low, high):
    gain, own = 1.0, jax.random.fold_in(rng, 6)
    for axis_at, parts in shards:
        draws = jnp.exp(jax.random.uniform(jax.random.fold_in(own, axis_at), (parts,), jnp.float32, low / len(shards), high / len(shards)))
        gain = gain * jnp.repeat(draws, shape[axis_at] // parts).reshape([-1 if axis == axis_at else 1 for axis in range(len(shape))])
    return gain


def deal_out(rng, own, number, rows, count, top, most, slope):
    ranking = jax.random.permutation(rng, count)
    crowded, common = shares(count, rows * top, most, slope, True), shares(count, rows * top, most, slope, False)
    places = jnp.arange(count)

    def named(tallies, offset_by):
        used = int((tallies > 0).sum())
        fixed = max(1, used // 4)
        moved = fixed + (places - fixed + offset_by * (used - fixed)) % max(1, count - fixed)
        return jnp.zeros((count,), jnp.int32).at[ranking[jnp.where(places < fixed, places, moved)]].set(jnp.asarray(tallies, jnp.int32))

    tallies = jnp.where(number % 4 == 0, named(crowded, number // 4), named(common, number - number // 4 - 1))
    mixed = jax.random.permutation(jax.random.fold_in(own, 3), count)
    donor, receiver = mixed[0:count // 2 * 2:2], mixed[1:count // 2 * 2:2]
    margin = jnp.minimum(tallies[donor] - 1, most - tallies[receiver]) // 2
    margin = jnp.where((donor == ranking[0]) | (receiver == ranking[0]) | (tallies[receiver] == 0), 0, jnp.maximum(margin, 0))
    moved = jax.random.randint(jax.random.fold_in(own, 4), (count // 2,), 0, 1 << 20) % (margin + 1)
    tallies = tallies.at[donor].add(-moved).at[receiver].add(moved)
    members = jnp.searchsorted(jnp.cumsum(tallies), jnp.arange(rows * top), side="right").astype(jnp.int32)
    grid = members.reshape(top, rows).T
    grid = grid[jax.random.permutation(jax.random.fold_in(own, 1), rows)]
    offset_by = jax.random.randint(jax.random.fold_in(own, 2), (rows, 1), 0, top)
    return jnp.take_along_axis(grid, (jnp.arange(top)[None, :] + offset_by) % top, axis=1)


def shares(amount, total, bound, lean, full):
    weights = [(1 << 20) // math.isqrt(grade ** lean) + 1 for grade in range(1, amount + 1)]
    largest = bound if full else min(bound, max(-(-total // amount), total * weights[0] // sum(weights)))
    least = 1 if total - largest >= amount - 1 else 0
    holding, spare = [largest] + [least] * (amount - 1), total - largest - least * (amount - 1)
    while spare > 0:
        movable = [i for i in range(1, amount) if holding[i] < largest] or [i for i in range(1, amount) if holding[i] < bound]
        whole, remaining = sum([weights[i] for i in movable]), spare
        for i in movable:
            addition = min(bound - holding[i], max(1, remaining * weights[i] // whole), spare)
            holding[i] = holding[i] + addition
            spare = spare - addition
    return np.array(holding)


def centred(rng, dims, scale, most, split=(), kind=jnp.bfloat16):
    gain = block_scale(rng, dims, split, -0.22, 0.18) if split else 1.0
    result = jax.random.normal(rng, dims, jnp.float32) * scale * gain
    return jnp.minimum(jnp.maximum(result, -most), most).astype(kind)


def setup_inputs(seed: int = 0) -> dict:
    arg_keys = jax.random.split(jax.random.key(seed), 28)
    tokens = centred(arg_keys[0], (TOKENS, D), 1.0, 6.0, ((0, 32),))
    teacher = centred(arg_keys[1], (TOKENS, D), 1.0, 6.0, ((0, 32),))
    attn_routes_keys = jax.random.split(jax.random.fold_in(arg_keys[2], 1), TOKENS // TOK_DEV)
    attn_routes_turns = jax.random.permutation(jax.random.fold_in(arg_keys[2], 3), TOKENS // TOK_DEV)
    attn_routes = jax.vmap(lambda own, number: deal_out(jax.random.fold_in(arg_keys[2], 2), own, number, TOK_DEV, EXPERTS, TOP, CAP, 1))(attn_routes_keys, attn_routes_turns).reshape((TOKENS, TOP))
    mlp_routes_keys = jax.random.split(jax.random.fold_in(arg_keys[3], 1), TOKENS // TOK_DEV)
    mlp_routes_turns = jax.random.permutation(jax.random.fold_in(arg_keys[3], 3), TOKENS // TOK_DEV)
    mlp_routes = jax.vmap(lambda own, number: deal_out(jax.random.fold_in(arg_keys[3], 2), own, number, TOK_DEV, EXPERTS, TOP, CAP, 1))(mlp_routes_keys, mlp_routes_turns).reshape((TOKENS, TOP))
    image_mask = draw_image_mask(jax.random.fold_in(arg_keys[27], 71), 0)
    valid = draw_valid(jax.random.fold_in(arg_keys[27], 71), 0)
    master_query = centred(arg_keys[6], (D, EXPERTS * QW), D ** -0.5, 0.125, ((0, 8), (1, 4)), jnp.float32)
    moment_query = centred(arg_keys[7], (D, EXPERTS * QW), (0.2 / TOKENS ** 0.5), 0.01875, ((0, 8), (1, 4)), jnp.float32)
    square_query = jnp.clip(jnp.exp(math.log(0.0001953125) - 2.3025851 * jax.random.uniform(arg_keys[8], (D, EXPERTS * QW), jnp.float32) ** block_scale(arg_keys[8], (D, EXPERTS * QW), ((0, 8), (1, 4)), -0.2, 0.2)), 1.9531249563442543e-05, 0.0001953125)
    master_project = centred(arg_keys[9], (EXPERTS * QW, D), (QW // 16) ** -0.5, 0.5, ((0, 4), (1, 8)), jnp.float32)
    moment_project = centred(arg_keys[10], (EXPERTS * QW, D), (0.055 / TOKENS ** 0.5), 0.00515625, ((0, 4), (1, 8)), jnp.float32)
    square_project = jnp.clip(jnp.exp(math.log(1.4648437172581907e-05) - 2.3025851 * jax.random.uniform(arg_keys[11], (EXPERTS * QW, D), jnp.float32) ** block_scale(arg_keys[11], (EXPERTS * QW, D), ((0, 4), (1, 8)), -0.2, 0.2)), 1.4648437627329258e-06, 1.4648437172581907e-05)
    master_gate_up = centred(arg_keys[12], (2, D, EXPERTS * FF), D ** -0.5, 0.125, ((1, 8), (2, 4)), jnp.float32)
    moment_gate_up = centred(arg_keys[13], (2, D, EXPERTS * FF), (0.08 / TOKENS ** 0.5), 0.0075, ((1, 8), (2, 4)), jnp.float32)
    square_gate_up = jnp.clip(jnp.exp(math.log(3.125000148429535e-05) - 2.3025852 * jax.random.uniform(arg_keys[14], (2, D, EXPERTS * FF), jnp.float32) ** block_scale(arg_keys[14], (2, D, EXPERTS * FF), ((1, 8), (2, 4)), -0.2, 0.2)), 3.12499992105586e-06, 3.125000148429535e-05)
    master_down = centred(arg_keys[15], (EXPERTS * FF, D), (FF // 2) ** -0.5, 0.109375, ((0, 4), (1, 8)), jnp.float32)
    moment_down = centred(arg_keys[16], (EXPERTS * FF, D), (0.11 / TOKENS ** 0.5), 0.0103125, ((0, 4), (1, 8)), jnp.float32)
    square_down = jnp.clip(jnp.exp(math.log(5.859374869032763e-05) - 2.3025851 * jax.random.uniform(arg_keys[17], (EXPERTS * FF, D), jnp.float32) ** block_scale(arg_keys[17], (EXPERTS * FF, D), ((0, 4), (1, 8)), -0.2, 0.2)), 5.859375050931703e-06, 5.859374869032763e-05)
    master_key_value = centred(arg_keys[18], (D, 2 * QW), D ** -0.5, 0.125, ((0, 32),), jnp.float32)
    moment_key_value = centred(arg_keys[19], (D, 2 * QW), (0.86 / TOKENS ** 0.5), 0.080625, ((0, 32),), jnp.float32)
    square_key_value = jnp.clip(jnp.exp(math.log(0.0036621094) - 2.3025851 * jax.random.uniform(arg_keys[20], (D, 2 * QW), jnp.float32) ** block_scale(arg_keys[20], (D, 2 * QW), ((0, 32),), -0.2, 0.2)), 0.00036621094, 0.0036621094)
    master_router = centred(arg_keys[21], (D, 2 * EXPERTS), (2 * D) ** -0.5, 0.09375, ((0, 32),), jnp.float32)
    moment_router = centred(arg_keys[22], (D, 2 * EXPERTS), (24.0 / TOKENS ** 0.5), 2.25, ((0, 32),), jnp.float32)
    square_router = jnp.clip(jnp.exp(math.log(2.8076172) - 2.3025851 * jax.random.uniform(arg_keys[23], (D, 2 * EXPERTS), jnp.float32) ** block_scale(arg_keys[23], (D, 2 * EXPERTS), ((0, 32),), -0.2, 0.2)), 0.28076172, 2.8076172)
    master_gains = jnp.clip(1.0 + 0.1 * jax.random.normal(arg_keys[24], (2, D), jnp.float32), 0.5, 1.5)
    moment_gains = centred(arg_keys[25], (2, D), 0.1, 0.6, ((1, 32),), jnp.float32)
    square_gains = jnp.clip(jnp.exp(math.log(0.2) - 2.3025851 * jax.random.uniform(arg_keys[26], (2, D), jnp.float32) ** block_scale(arg_keys[26], (2, D), ((1, 32),), -0.2, 0.2)), 0.02, 0.2)
    return {"tokens": tokens, "teacher": teacher, "attn_routes": attn_routes, "mlp_routes": mlp_routes, "image_mask": image_mask, "valid": valid, "master_query": master_query, "moment_query": moment_query, "square_query": square_query, "master_project": master_project, "moment_project": moment_project, "square_project": square_project, "master_gate_up": master_gate_up, "moment_gate_up": moment_gate_up, "square_gate_up": square_gate_up, "master_down": master_down, "moment_down": moment_down, "square_down": square_down, "master_key_value": master_key_value, "moment_key_value": moment_key_value, "square_key_value": square_key_value, "master_router": master_router, "moment_router": moment_router, "square_router": square_router, "master_gains": master_gains, "moment_gains": moment_gains, "square_gains": square_gains}


@jax.custom_vjp
def low(v):
    return lax.optimization_barrier(v.astype(jnp.bfloat16)).astype(jnp.float32)

@jax.custom_vjp
def low_back(v):
    return v

def low_keep(v):
    return (low(v), None)

def low_pass(kept, grad):
    return (grad,)

def back_keep(v):
    return (v, None)

def back_low(kept, grad):
    return (low(grad),)
low.defvjp(low_keep, low_pass)
low_back.defvjp(back_keep, back_low)
NORM_EPS = 1e-05
ADAM_EPS = 1e-08
BETA_FIRST = 0.9
BETA_SECOND = 0.95
ROPE_BASE = 10000.0
MASK_FILL = -1000000000.0
HIGHEST = lax.Precision.HIGHEST

def rope_tables():
    half_dim = HD // 2
    frequency = ROPE_BASE ** (-(2.0 * jnp.arange(half_dim, dtype=jnp.float32)) / HD)
    angles = jnp.arange(TOK_DEV, dtype=jnp.float32)[:, None] * frequency[None, :]
    return (jnp.cos(angles), jnp.sin(angles))

def rotate(values, cosine_table, sine_table):
    half_dim = values.shape[-1] // 2
    lower_half = values[..., :half_dim]
    upper_half = values[..., half_dim:]
    cos_wide = cosine_table[:, None, :]
    sin_wide = sine_table[:, None, :]
    return jnp.concatenate([lower_half * cos_wide - upper_half * sin_wide, upper_half * cos_wide + lower_half * sin_wide], axis=-1)

def rms_norm(values, gain_row):
    inverse = lax.rsqrt(lax.optimization_barrier(jnp.mean(values * values, axis=-1, keepdims=True)) + NORM_EPS)
    return values * inverse * gain_row

def chosen_gates(logits, routes):
    picked = jnp.take_along_axis(logits, routes, axis=-1)
    return jax.nn.softmax(picked, axis=-1)

def expert_hits(routes):
    return (routes[:, :, None] == jnp.arange(EXPERTS, dtype=jnp.int32)[None, None, :]).astype(jnp.float32)

def group_forward(weights, rows_x, routes_attn, routes_mlp, image_rows):
    query_w, project_w, gate_up_w, down_w, key_value_w, router_w, gains_w = weights
    row_count = rows_x.shape[0]
    seq_count = row_count // TOK_DEV
    cosine_table, sine_table = rope_tables()
    normed = low(rms_norm(rows_x, gains_w[0]))
    kv_proj = low_back(jnp.dot(normed, key_value_w, precision=HIGHEST))
    key_rows = low(rotate(kv_proj[:, :QW].reshape(seq_count, TOK_DEV, HEADS, HD), cosine_table, sine_table))
    value_rows = low(kv_proj[:, QW:].reshape(seq_count, TOK_DEV, HEADS, HD))
    gates_attn = chosen_gates(jnp.dot(normed, router_w[:, :EXPERTS], precision=HIGHEST), routes_attn)
    hits_attn = expert_hits(routes_attn)
    expert_ids = jnp.arange(EXPERTS, dtype=jnp.int32)

    def query_step(running, expert):
        weight_block = lax.dynamic_slice_in_dim(query_w, expert * QW, QW, 1)
        produced = jnp.dot(normed, weight_block, precision=HIGHEST)
        picked = lax.dynamic_index_in_dim(hits_attn, expert, 2, keepdims=False)
        return (running + picked[:, :, None] * produced[:, None, :], None)
    query_sum, unused = lax.scan(jax.checkpoint(query_step), jnp.zeros((row_count, TOP, QW), jnp.float32), expert_ids)
    query_pre = low_back(query_sum)
    queries = low(rotate(query_pre.reshape(seq_count, TOK_DEV, TOP * HEADS, HD), cosine_table, sine_table))
    queries = queries.reshape(seq_count, TOK_DEV, TOP, HEADS, HD)
    scores = jnp.einsum('gqjhd,gkhd->gjhqk', queries, key_rows, precision=HIGHEST) * HD ** (-0.5)
    image_on = image_rows.reshape(seq_count, TOK_DEV) > 0
    position = jnp.arange(TOK_DEV, dtype=jnp.int32)
    allowed = (position[None, :, None] >= position[None, None, :]) | image_on[:, :, None] & image_on[:, None, :]
    scores = low_back(jnp.where(allowed[:, None, None], scores, MASK_FILL))
    prob_table = jax.nn.softmax(scores, axis=-1)
    attended = jnp.einsum('gjhqk,gkhd->gqjhd', low(prob_table), value_rows, precision=HIGHEST)
    attended = low(low_back(attended)).reshape(row_count, TOP, QW)

    def project_step(running, expert):
        weight_block = lax.dynamic_slice_in_dim(project_w, expert * QW, QW, 0)
        picked = lax.dynamic_index_in_dim(hits_attn, expert, 2, keepdims=False)
        produced = jnp.einsum('rjq,qd->rjd', attended * picked[:, :, None], weight_block, precision=HIGHEST)
        return (running + produced, None)
    project_sum, unused = lax.scan(jax.checkpoint(project_step), jnp.zeros((row_count, TOP, D), jnp.float32), expert_ids)
    branch = low_back(project_sum)
    hidden = rows_x + lax.optimization_barrier(jnp.sum(gates_attn[:, :, None] * branch, axis=1))
    normed_two = low(rms_norm(hidden, gains_w[1]))
    gates_mlp = chosen_gates(jnp.dot(normed_two, router_w[:, EXPERTS:], precision=HIGHEST), routes_mlp)
    hits_mlp = expert_hits(routes_mlp)

    def mlp_step(running, expert):
        gate_block = lax.dynamic_slice_in_dim(gate_up_w[0], expert * FF, FF, 1)
        up_block = lax.dynamic_slice_in_dim(gate_up_w[1], expert * FF, FF, 1)
        down_block = lax.dynamic_slice_in_dim(down_w, expert * FF, FF, 0)
        gate_val = low_back(jnp.dot(normed_two, gate_block, precision=HIGHEST))
        up_val = low_back(jnp.dot(normed_two, up_block, precision=HIGHEST))
        active = low(jax.nn.silu(gate_val) * up_val)
        produced = jnp.dot(active, down_block, precision=HIGHEST)
        picked = lax.dynamic_index_in_dim(hits_mlp, expert, 2, keepdims=False)
        return (running + picked[:, :, None] * produced[:, None, :], None)
    mlp_sum, unused = lax.scan(jax.checkpoint(mlp_step), jnp.zeros((row_count, TOP, D), jnp.float32), expert_ids)
    mlp_branch = low_back(mlp_sum)
    return hidden + lax.optimization_barrier(jnp.sum(gates_mlp[:, :, None] * mlp_branch, axis=1))

def total_loss(masters, tokens_f, teacher_f, attn_routes, mlp_routes, image_mask, valid_f, valid_count):
    weights = tuple((low(master) for master in masters))
    seq_total = TOKENS // TOK_DEV
    rows_group = TOK_DEV * min(seq_total, max(1, 4096 // TOK_DEV))
    groups = TOKENS // rows_group

    def one_group(running, inputs):
        rows_x, rows_attn, rows_mlp, rows_image, rows_valid, rows_teacher = inputs
        out_rows = jax.checkpoint(group_forward)(weights, rows_x, rows_attn, rows_mlp, rows_image)
        deviation = out_rows - rows_teacher
        return (running + jnp.sum(rows_valid[:, None] * deviation * deviation), out_rows)
    stacked = tuple((array_in.reshape((groups, rows_group) + array_in.shape[1:]) for array_in in (tokens_f, attn_routes, mlp_routes, image_mask, valid_f, teacher_f)))
    loss_sum, outputs = lax.scan(one_group, jnp.zeros((), jnp.float32), stacked)
    return (loss_sum / valid_count, outputs.reshape(TOKENS, D))

def adam_step(moment, square, gradient):
    moment_new = BETA_FIRST * moment + (1.0 - BETA_FIRST) * gradient
    square_new = BETA_SECOND * square + (1.0 - BETA_SECOND) * gradient * gradient
    moment_hat = moment_new / (1.0 - BETA_FIRST ** STEP)
    square_hat = square_new / (1.0 - BETA_SECOND ** STEP)
    direction = moment_hat / (jnp.sqrt(square_hat) + ADAM_EPS)
    return (direction, moment_new, square_new)

def reference(tokens, teacher, attn_routes, mlp_routes, image_mask, valid, master_query, moment_query, square_query, master_project, moment_project, square_project, master_gate_up, moment_gate_up, square_gate_up, master_down, moment_down, square_down, master_key_value, moment_key_value, square_key_value, master_router, moment_router, square_router, master_gains, moment_gains, square_gains):
    masters = (master_query, master_project, master_gate_up, master_down, master_key_value, master_router, master_gains)
    moments = (moment_query, moment_project, moment_gate_up, moment_down, moment_key_value, moment_router, moment_gains)
    squares = (square_query, square_project, square_gate_up, square_down, square_key_value, square_router, square_gains)
    valid_f = valid.astype(jnp.float32)
    valid_count = jnp.sum(valid_f)
    teacher_f = teacher.astype(jnp.float32)

    def loss_of(master_set, tokens_f):
        return total_loss(master_set, tokens_f, teacher_f, attn_routes, mlp_routes, image_mask, valid_f, valid_count)
    loss_value, pullback, outputs = jax.vjp(loss_of, masters, tokens.astype(jnp.float32), has_aux=True)
    gradients, input_grad = pullback(jnp.ones((), jnp.float32))
    upd = [adam_step(moments[index], squares[index], gradients[index]) for index in range(7)]
    return (outputs, loss_value, input_grad, gradients[0], upd[0][0], upd[0][1], upd[0][2], gradients[1], upd[1][0], upd[1][1], upd[1][2], gradients[2], upd[2][0], upd[2][1], upd[2][2], gradients[3], upd[3][0], upd[3][1], upd[3][2], gradients[4], upd[4][0], upd[4][1], upd[4][2], gradients[5], upd[5][0], upd[5][1], upd[5][2], gradients[6], upd[6][0], upd[6][1], upd[6][2])
```

```python
import jax
import jax.numpy as jnp
from jax import lax
from jax.sharding import PartitionSpec as P

D = 2048
HD = 128
EXPERTS = 4
TOP = 2
STEP = 10
QW = 2048
CAP = 96
LANES = 128

NORM_EPS = 1e-05
ADAM_EPS = 1e-08
BETA_FIRST = 0.9
BETA_SECOND = 0.95
ROPE_BASE = 10000.0
MASK_FILL = -1000000000.0
SCALE = HD ** (-0.5)
HIGHEST = lax.Precision.HIGHEST
F32 = jnp.float32
BF16 = jnp.bfloat16


def matmul(left_side, right_side):
    return jnp.dot(left_side, right_side, preferred_element_type=F32)


def matmul_back(left_side, right_side):
    return lax.dot_general(
        left_side, right_side, (((1,), (1,)), ((), ())), preferred_element_type=F32
    )


def matmul_rows(left_side, right_side):
    return lax.dot_general(
        left_side, right_side, (((0,), (0,)), ((), ())), preferred_element_type=F32
    )


def exact_back(left_side, right_side):
    return lax.dot_general(
        left_side,
        right_side,
        (((1,), (1,)), ((), ())),
        precision=HIGHEST,
        preferred_element_type=F32,
    )


def exact_rows(left_side, right_side):
    return lax.dot_general(
        left_side,
        right_side,
        (((0,), (0,)), ((), ())),
        precision=HIGHEST,
        preferred_element_type=F32,
    )


def rope_tables(length):
    half_dim = HD // 2
    frequency = ROPE_BASE ** (-(2.0 * jnp.arange(half_dim, dtype=F32)) / HD)
    angles = jnp.arange(length, dtype=F32)[:, None] * frequency[None, :]
    cosine, sine = jnp.cos(angles), jnp.sin(angles)
    return (
        jnp.concatenate([cosine, cosine], axis=1),
        jnp.concatenate([-sine, sine], axis=1),
    )


def swap_perm(count, bits):
    return [(place, place ^ bits) for place in range(count)]


def core_swap(value):
    return lax.ppermute(value, "dp", swap_perm(lax.axis_size("dp"), 1))


def over_expert(value, bits):
    if bits == 0:
        return value
    return lax.ppermute(value, "expert", swap_perm(lax.axis_size("expert"), bits))


def chip_groups():
    count = lax.axis_size("dp")
    return [[2 * place + core for place in range(count // 2)] for core in range(2)]


def gather_chips(block):
    return lax.all_gather(block, "dp", axis=0, tiled=True, axis_index_groups=chip_groups())


def scatter_chips(partial):
    return lax.psum_scatter(
        partial, "dp", scatter_dimension=0, tiled=True, axis_index_groups=chip_groups()
    )


def in_core_order(core, mine, other, axis):
    return jnp.where(
        core == 0,
        jnp.concatenate([mine, other], axis=axis),
        jnp.concatenate([other, mine], axis=axis),
    )


def stack_rows(core, mine, got):
    both = jnp.concatenate([mine, mine], axis=0)
    return lax.dynamic_update_slice_in_dim(both, got, (1 - core) * mine.shape[0], 0)


def halves_of(core, whole):
    width = whole.shape[-1] // 2
    low, high = whole[..., :width], whole[..., width:]
    return (jnp.where(core == 0, low, high), jnp.where(core == 0, high, low))


def exchange_rows(core, summed):
    rows = summed.shape[0] // 2
    low, high = summed[:rows], summed[rows:]
    mine = jnp.where(core == 0, low, high)
    return (mine, core_swap(jnp.where(core == 0, high, low)))


def slots_before(hits):
    count = hits.shape[-2]
    place = jnp.arange(count, dtype=jnp.int32)
    earlier = (place[:, None] > place[None, :]).astype(BF16)
    return jnp.einsum(
        "ts,...sn->...tn", earlier, hits.astype(BF16), preferred_element_type=F32
    ).astype(jnp.int32)


def route_tables(routes, names):
    hit = routes[:, :, None] == names[None, None, :]
    named = jnp.any(hit, axis=1)
    slot = slots_before(named)
    at_slot = slot[:, :, None] == jnp.arange(CAP, dtype=jnp.int32)[None, None, :]
    pick = (named[:, :, None] & at_slot).astype(BF16).transpose(1, 2, 0)
    back = (hit[:, :, :, None] & at_slot[:, None]).astype(BF16)
    back = back.transpose(1, 0, 2, 3).reshape(TOP, routes.shape[0], -1)
    return (pick, back, hit.astype(F32))


def chosen_gates(logits, routes):
    hit = routes[:, :, None] == jnp.arange(EXPERTS, dtype=jnp.int32)[None, None, :]
    picked = jnp.sum(jnp.where(hit, logits[:, None, :], 0.0), axis=2)
    return jax.nn.softmax(picked, axis=-1)


def gate_back(gates, grad_gates, routes):
    hit = routes[:, :, None] == jnp.arange(EXPERTS, dtype=jnp.int32)[None, None, :]
    centred = gates * (grad_gates - jnp.sum(gates * grad_gates, axis=-1, keepdims=True))
    return jnp.sum(centred[:, :, None] * hit.astype(F32), axis=1)


def norm_back(values, inverse, gain_row, grad_normed):
    scaled = gain_row * grad_normed
    grad_values = inverse * scaled - values * inverse**3 * jnp.mean(
        scaled * values, axis=-1, keepdims=True
    )
    grad_gain = jnp.sum(grad_normed * values * inverse, axis=0)
    return (grad_values, grad_gain)


def send_rows(blocks):
    got = jnp.concatenate([over_expert(block, bits) for bits, block in enumerate(blocks)])
    return jnp.concatenate([got, core_swap(got)])


def return_rows(partial, partners):
    count = partial.shape[0] // 2
    got = core_swap(partial[count:].astype(BF16))
    summed = (partial[:count] + got.astype(F32)).astype(BF16)
    summed = summed.reshape((partners, count // partners) + summed.shape[1:])
    return [over_expert(summed[bits], bits) for bits in range(partners)]


def rotate(value, cosine, sine):
    half_dim = HD // 2
    swapped = jnp.concatenate([value[..., half_dim:], value[..., :half_dim]], axis=-1)
    return value * cosine + swapped * sine


def by_heads(rows, sequences):
    return rows.reshape(sequences, -1, rows.shape[1] // HD, HD).transpose(0, 2, 1, 3)


def from_heads(blocks):
    sequences, heads, tokens, _ = blocks.shape
    return blocks.transpose(0, 2, 1, 3).reshape(sequences * tokens, heads * HD)


def heads_dot(left_side, right_side, left_axis, right_axis):
    return lax.dot_general(
        left_side,
        right_side,
        (((left_axis,), (right_axis,)), ((0, 1), (0, 1))),
        preferred_element_type=F32,
    )


def xor_blocks(value, axis, bits):
    count, step = value.shape[axis], 1
    while step < count:
        if bits & step:
            split = value.shape[:axis] + (count // (2 * step), 2, step) + value.shape[axis + 1 :]
            value = jnp.flip(value.reshape(split), axis + 1).reshape(value.shape)
        step *= 2
    return value


def partner_columns(expert, rows):
    width = rows.shape[1] // EXPERTS
    return jnp.concatenate(
        [
            lax.dynamic_slice_in_dim(rows, (expert ^ at) * width, width, 1)
            for at in range(EXPERTS)
        ],
        axis=1,
    )


def all_sum(value):
    bits = 1
    while bits < lax.axis_size("dp"):
        value = value + lax.ppermute(value, "dp", swap_perm(lax.axis_size("dp"), bits))
        bits *= 2
    bits = 1
    while bits < lax.axis_size("expert"):
        value = value + over_expert(value, bits)
        bits *= 2
    return value


def after(value, *others):
    return lax.optimization_barrier((value, *others))[0]


def adam_step(moment, square, gradient):
    moment_new = BETA_FIRST * moment + (1.0 - BETA_FIRST) * gradient
    square_new = BETA_SECOND * square + (1.0 - BETA_SECOND) * gradient * gradient
    moment_hat = moment_new / (1.0 - BETA_FIRST**STEP)
    square_hat = square_new / (1.0 - BETA_SECOND**STEP)
    direction = moment_hat / (jnp.sqrt(square_hat) + ADAM_EPS)
    return (gradient, direction, moment_new, square_new)


def body(
    tokens,
    teacher,
    attn_routes,
    mlp_routes,
    image_mask,
    valid,
    master_query,
    moment_query,
    square_query,
    master_project,
    moment_project,
    square_project,
    master_gate_up,
    moment_gate_up,
    square_gate_up,
    master_down,
    moment_down,
    square_down,
    master_key_value,
    moment_key_value,
    square_key_value,
    master_router,
    moment_router,
    square_router,
    master_gains,
    moment_gains,
    square_gains,
):
    partners = lax.axis_size("expert")
    halves = partners // EXPERTS
    core = lax.axis_index("dp") % 2
    expert_at = lax.axis_index("expert")
    expert, half = expert_at // halves, expert_at % halves
    names = (expert_at ^ jnp.arange(partners, dtype=jnp.int32)) // halves
    token_count = tokens.shape[0]
    sequences = 2 * partners
    sixth = master_query.shape[1] // (2 * EXPERTS)

    valid_f = valid.astype(F32)
    marks = jnp.concatenate([attn_routes, image_mask[:, None]], axis=1).astype(BF16)
    marks = jnp.pad(marks, ((0, 0), (0, LANES - marks.shape[1])))
    payload = jnp.concatenate([tokens, marks], axis=1)
    everyone = send_rows([payload] * partners)

    query_mine, query_theirs = halves_of(core, master_query.astype(BF16))
    project_mine, project_theirs = halves_of(core, master_project.astype(BF16).T)
    attn_got = core_swap(jnp.concatenate([query_theirs, project_theirs], axis=1))
    attn_mine = jnp.concatenate([query_mine, project_mine], axis=1)
    width_attn = query_mine.shape[1]

    def arranged(rows):
        return jnp.concatenate(
            [
                partner_columns(expert, rows[:, :width_attn]),
                partner_columns(expert, rows[:, width_attn:]),
            ],
            axis=1,
        )

    weight_attn = gather_chips(stack_rows(core, arranged(attn_mine), arranged(attn_got)))
    weight_query, weight_project = weight_attn[:, :width_attn], weight_attn[:, width_attn:]

    local_rows = master_key_value.shape[0]
    shared_low = master_key_value.astype(BF16).reshape(local_rows, 2, halves, 2, EXPERTS, sixth)
    small = jnp.concatenate(
        [
            master_router,
            master_gains.T,
            jnp.full((local_rows, 1), jnp.sum(valid_f)),
        ],
        axis=1,
    ).astype(BF16)
    small = jnp.pad(small, ((0, 0), (0, LANES - small.shape[1])))
    for_cores = [
        jnp.concatenate([shared_low[:, :, :, at].reshape(local_rows, -1), small], axis=1)
        for at in range(2)
    ]
    pair = jnp.stack(
        [
            jnp.where(core == 0, for_cores[0], for_cores[1]),
            core_swap(jnp.where(core == 0, for_cores[1], for_cores[0])),
        ]
    )
    pair_kv = pair[:, :, :-LANES].reshape(2, local_rows, 2, halves * EXPERTS, sixth)

    def block_for(bits):
        other = expert_at ^ bits
        column = (other % halves) * EXPERTS + other // halves
        picked = lax.dynamic_index_in_dim(pair_kv, column, 3, keepdims=False)
        return jnp.concatenate([picked.reshape(2, local_rows, -1), pair[:, :, -LANES:]], axis=2)

    arrived = jnp.stack([over_expert(block_for(bits), bits) for bits in range(partners)])
    arrived = jnp.stack(
        [lax.dynamic_index_in_dim(arrived, expert_at ^ at, 0, keepdims=False) for at in range(partners)]
    )
    arrived = jnp.where(core == 0, arrived, arrived[:, ::-1]).transpose(1, 0, 2, 3)
    shared_whole = gather_chips(arrived.reshape(2 * partners * local_rows, -1))
    kv_weight = shared_whole[:, : 2 * sixth]
    small_whole = shared_whole[:, 2 * sixth :]
    router_low = small_whole[:, : 2 * EXPERTS]
    router_f = router_low.astype(F32)
    gains_f = small_whole[:, 2 * EXPERTS : 2 * EXPERTS + 2].astype(F32).T
    total_count = jnp.sum(small_whole[:, 2 * EXPERTS + 2].astype(F32)) / local_rows

    width_ff = master_gate_up.shape[2] // 2
    gate_mine, gate_theirs = halves_of(core, master_gate_up[0].astype(BF16))
    up_mine, up_theirs = halves_of(core, master_gate_up[1].astype(BF16))
    gate_up_got = core_swap(jnp.concatenate([gate_theirs, up_theirs], axis=1))
    weight_gate_up = gather_chips(
        stack_rows(core, jnp.concatenate([gate_mine, up_mine], axis=1), gate_up_got)
    )
    down_mine, down_theirs = halves_of(core, master_down.astype(BF16).T)
    weight_down = gather_chips(stack_rows(core, down_mine, core_swap(down_theirs)))

    tables = rope_tables(token_count)
    inputs_all = everyone[:, :D].astype(F32)
    inverse_all = lax.rsqrt(jnp.mean(inputs_all * inputs_all, axis=-1, keepdims=True) + NORM_EPS)
    normed_all = (inputs_all * inverse_all * gains_f[0]).astype(BF16)
    inputs_f = tokens.astype(F32)
    inverse_one, normed_one = inverse_all[:token_count], normed_all[:token_count]
    marks_all = everyone[:, D:].astype(F32).reshape(sequences, token_count, LANES)
    named_all = jnp.any(marks_all[:, :, :TOP] == expert.astype(F32), axis=2)
    slot_all = slots_before(named_all[:, :, None])[:, :, 0]
    slots = jnp.arange(CAP, dtype=jnp.int32)
    pick_all = (named_all[:, None, :] & (slot_all[:, None, :] == slots[None, :, None])).astype(BF16)
    image_on = marks_all[:, :, TOP] > 0.0
    position = jnp.arange(token_count, dtype=jnp.int32)
    allowed = (position[:, None] >= position[None, :])[None] | (
        image_on[:, :, None] & image_on[:, None, :]
    )

    def regroup(rows, bits):
        blocks = rows.reshape((2, partners, token_count) + rows.shape[1:])
        return xor_blocks(blocks, 1, bits).reshape(rows.shape)

    kv_proj = matmul(normed_all, kv_weight)
    key_own = rotate(by_heads(kv_proj[:, :sixth], sequences), *tables).astype(BF16)
    kv_own = jnp.concatenate([from_heads(key_own), kv_proj[:, sixth:].astype(BF16)], axis=1)
    kv_shared = [
        regroup(over_expert(kv_own, step * halves), step * halves) for step in range(EXPERTS)
    ]
    key_heads = by_heads(jnp.concatenate([part[:, :sixth] for part in kv_shared], axis=1), sequences)
    value_heads = by_heads(
        jnp.concatenate([part[:, sixth:] for part in kv_shared], axis=1), sequences
    )
    query_pre = matmul(normed_all, weight_query)
    query_heads = rotate(by_heads(query_pre, sequences), *tables).astype(BF16)
    scores = heads_dot(query_heads, key_heads, 3, 3) * SCALE
    scores = jnp.where(allowed[:, None], scores, MASK_FILL)
    probs = jax.nn.softmax(scores, axis=-1)
    probs_low = probs.astype(BF16)
    attended_all = from_heads(heads_dot(probs_low, value_heads, 3, 2).astype(BF16))

    def per_sequence(table, rows, left_axis):
        blocks = rows.reshape(sequences, -1, rows.shape[1])
        picked = lax.dot_general(
            table, blocks, (((left_axis,), (1,)), ((0,), (0,))), preferred_element_type=F32
        )
        return picked.astype(BF16).reshape(-1, rows.shape[1])

    attended = per_sequence(pick_all, attended_all, 2)

    attn_pick, attn_back, attn_hit = route_tables(attn_routes, names)
    gates_attn = chosen_gates(matmul(normed_one, router_low[:, :EXPERTS]), attn_routes)
    branch_rows = jnp.concatenate(
        return_rows(matmul_back(attended, weight_project), partners)
    )
    branch = [matmul(attn_back[choice], branch_rows) for choice in range(TOP)]
    hidden = inputs_f + sum(gates_attn[:, choice, None] * branch[choice] for choice in range(TOP))

    inverse_two = lax.rsqrt(jnp.mean(hidden * hidden, axis=-1, keepdims=True) + NORM_EPS)
    normed_two = (hidden * inverse_two * gains_f[1]).astype(BF16)
    mlp_pick, mlp_back, mlp_hit = route_tables(mlp_routes, names)
    gates_mlp = chosen_gates(matmul(normed_two, router_low[:, EXPERTS:]), mlp_routes)
    placed = matmul(mlp_pick.reshape(-1, token_count), normed_two).astype(BF16)
    rows_two = send_rows(list(placed.reshape(partners, CAP, D)))
    gate_up_val = matmul(rows_two, weight_gate_up)
    gate_val, up_val = gate_up_val[:, :width_ff], gate_up_val[:, width_ff:]
    active = (jax.nn.silu(gate_val) * up_val).astype(BF16)
    mlp_rows = jnp.concatenate(return_rows(matmul_back(active, weight_down), partners))
    mlp_branch = [matmul(mlp_back[choice], mlp_rows) for choice in range(TOP)]
    outputs = hidden + sum(gates_mlp[:, choice, None] * mlp_branch[choice] for choice in range(TOP))

    deviation = outputs - teacher.astype(F32)
    local_error = jnp.sum(valid_f[:, None] * deviation * deviation)
    total_error = all_sum(local_error.reshape(1, 1))[0, 0]
    grad_out = 2.0 * valid_f[:, None] * deviation / total_count

    def send_grads(pick, gates, hit, grad):
        gate_of = jnp.sum(gates[:, :, None] * hit, axis=1)
        rows = (gate_of.T[:, :, None] * grad[None]).astype(BF16)
        sent = jnp.einsum("kct,ktd->kcd", pick, rows, preferred_element_type=F32).astype(BF16)
        return send_rows(list(sent))

    rows_grad = send_grads(mlp_pick, gates_mlp, mlp_hit, grad_out)
    grad_down = matmul_rows(rows_grad, active).astype(BF16)
    grad_active = matmul(rows_grad, weight_down)
    sigmoid_gate = jax.nn.sigmoid(gate_val)
    grad_gate = (
        grad_active * up_val * sigmoid_gate * (1.0 + gate_val * (1.0 - sigmoid_gate))
    ).astype(BF16)
    grad_up = (grad_active * gate_val * sigmoid_gate).astype(BF16)
    grad_both = jnp.concatenate([grad_gate, grad_up], axis=1)
    down_sum = scatter_chips(grad_down)
    grad_gate_up = matmul_rows(rows_two, grad_both).astype(BF16)
    gate_up_sum = scatter_chips(after(grad_gate_up, down_sum))
    normed_two_rows = return_rows(
        matmul_back(after(grad_both, grad_down), weight_gate_up), partners
    )
    grad_gates_mlp = jnp.stack(
        [jnp.sum(grad_out * mlp_branch[choice], axis=-1) for choice in range(TOP)], axis=1
    )
    grad_logits_mlp = gate_back(gates_mlp, grad_gates_mlp, mlp_routes)
    grad_normed_two = matmul(
        jnp.sum(mlp_back, axis=0), jnp.concatenate(normed_two_rows)
    ) + exact_back(grad_logits_mlp, router_f[:, EXPERTS:])
    grad_hidden_norm, grad_gain_two = norm_back(hidden, inverse_two, gains_f[1], grad_normed_two)
    grad_hidden = grad_out + grad_hidden_norm
    grad_router_two = exact_rows(normed_two.astype(F32), grad_logits_mlp)

    rows_grad_attn = send_grads(attn_pick, gates_attn, attn_hit, after(grad_hidden, down_sum))
    grad_project = matmul_rows(rows_grad_attn, attended).astype(BF16)
    grad_attended = matmul(rows_grad_attn, weight_project).astype(BF16)
    grad_gates_attn = jnp.stack(
        [jnp.sum(grad_hidden * branch[choice], axis=-1) for choice in range(TOP)], axis=1
    )
    grad_logits_attn = gate_back(gates_attn, grad_gates_attn, attn_routes)
    grad_heads = by_heads(per_sequence(pick_all, grad_attended, 1), sequences)
    grad_probs = heads_dot(grad_heads, value_heads, 3, 3)
    inner = jnp.sum(probs * grad_probs, axis=-1, keepdims=True)
    grad_scores = (probs * (grad_probs - inner)).astype(BF16)
    grad_query_heads = heads_dot(grad_scores, key_heads, 3, 2) * SCALE
    grad_key_heads = heads_dot(grad_scores, query_heads, 2, 2) * SCALE
    grad_value_heads = heads_dot(probs_low, grad_heads, 2, 2)
    back_tables = (tables[0], -tables[1])
    grad_query_pre = from_heads(rotate(grad_query_heads, *back_tables).astype(BF16))
    grad_keys = from_heads(rotate(grad_key_heads, *back_tables).astype(BF16))
    grad_values = from_heads(grad_value_heads.astype(BF16))
    grad_query = matmul_rows(normed_all, grad_query_pre).astype(BF16)
    grad_kv = sum(
        over_expert(
            regroup(
                jnp.concatenate(
                    [
                        grad_keys[:, step * sixth : (step + 1) * sixth],
                        grad_values[:, step * sixth : (step + 1) * sixth],
                    ],
                    axis=1,
                ),
                step * halves,
            ),
            step * halves,
        ).astype(F32)
        for step in range(EXPERTS)
    ).astype(BF16)
    grad_kv_weight = matmul_rows(normed_all, grad_kv).astype(BF16)
    normed_one_rows = return_rows(
        matmul_back(grad_query_pre, weight_query) + matmul_back(grad_kv, kv_weight), partners
    )
    grad_normed_one = sum(rows.astype(F32) for rows in normed_one_rows) + exact_back(
        grad_logits_attn, router_f[:, :EXPERTS]
    )
    grad_inputs_norm, grad_gain_one = norm_back(inputs_f, inverse_one, gains_f[0], grad_normed_one)
    input_grad = grad_hidden + grad_inputs_norm
    grad_small = jnp.concatenate(
        [
            exact_rows(normed_one.astype(F32), grad_logits_attn),
            grad_router_two,
            grad_gain_one[:, None],
            grad_gain_two[:, None],
        ],
        axis=1,
    ).astype(BF16)
    grad_small = jnp.pad(grad_small, ((0, 0), (0, LANES - grad_small.shape[1])))

    attn_sum = scatter_chips(
        after(
            jnp.concatenate([grad_query, grad_project, grad_kv_weight, grad_small], axis=1),
            gate_up_sum,
        )
    )
    down_mine, down_other = exchange_rows(core, down_sum)
    gate_up_mine, gate_up_other = exchange_rows(core, gate_up_sum)
    attn_mine, attn_other = exchange_rows(core, attn_sum[:, : 2 * width_attn])
    attn_mine, attn_other = arranged(attn_mine), arranged(attn_other)
    shared_sum = attn_sum[:, 2 * width_attn :]
    shared_sum = shared_sum.reshape(2, partners, local_rows, -1)
    shared_mine = jnp.where(core == 0, shared_sum[0], shared_sum[1])
    shared_theirs = core_swap(jnp.where(core == 0, shared_sum[1], shared_sum[0]))
    shared_pair = jnp.where(
        core == 0, jnp.stack([shared_mine, shared_theirs]), jnp.stack([shared_theirs, shared_mine])
    )
    received = jnp.stack(
        [
            over_expert(lax.dynamic_index_in_dim(shared_pair, expert_at ^ bits, 1, keepdims=False), bits)
            for bits in range(partners)
        ]
    )
    small_sum = jnp.sum(received[..., -LANES:].astype(F32), axis=(0, 1))
    received = jnp.stack(
        [lax.dynamic_index_in_dim(received, expert_at ^ at, 0, keepdims=False) for at in range(partners)]
    )
    reduced_kv = (
        received[..., :-LANES]
        .reshape(EXPERTS, halves, 2, local_rows, 2, sixth)
        .transpose(3, 4, 1, 2, 0, 5)
        .reshape(local_rows, -1)
        .astype(F32)
    )
    reduced_router = small_sum[:, : 2 * EXPERTS]
    reduced_gains = small_sum[:, 2 * EXPERTS : 2 * EXPERTS + 2].T
    reduced_query = in_core_order(
        core, attn_mine[:, :width_attn], attn_other[:, :width_attn], 1
    ).astype(F32)
    reduced_project = after(
        in_core_order(core, attn_mine[:, width_attn:], attn_other[:, width_attn:], 1).T
    ).astype(F32)
    reduced_down = after(in_core_order(core, down_mine, down_other, 1).T).astype(F32)
    reduced_gate_up = jnp.stack(
        [
            in_core_order(
                core,
                gate_up_mine[:, at * width_ff : (at + 1) * width_ff],
                gate_up_other[:, at * width_ff : (at + 1) * width_ff],
                1,
            )
            for at in range(2)
        ]
    ).astype(F32)
    loss_value = total_error / total_count
    return (
        outputs,
        loss_value,
        input_grad,
        *adam_step(moment_query, square_query, reduced_query),
        *adam_step(moment_project, square_project, reduced_project),
        *adam_step(moment_gate_up, square_gate_up, reduced_gate_up),
        *adam_step(moment_down, square_down, reduced_down),
        *adam_step(moment_key_value, square_key_value, reduced_kv),
        *adam_step(moment_router, square_router, reduced_router),
        *adam_step(moment_gains, square_gains, reduced_gains),
    )


def solution(mesh):
    rows = P(("dp", "expert"), None)
    flat = P(("dp", "expert"))
    columns = P(None, ("dp", "expert"))
    query, project, gate_up = P("dp", "expert"), P("expert", "dp"), P(None, "dp", "expert")
    weights = (query, project, gate_up, project, rows, rows, columns)
    return jax.shard_map(
        body,
        mesh=mesh,
        in_specs=(rows, rows, rows, rows, flat, flat)
        + tuple(spec for spec in weights for _ in range(3)),
        out_specs=(rows, P(), rows) + tuple(spec for spec in weights for _ in range(4)),
        check_vma=False,
    )
```

```python
import jax
import jax.numpy as jnp
from jax import lax
from jax.experimental.layout import Layout, with_layout_constraint
from jax.sharding import PartitionSpec as P

D = 2048
HD = 128
EXPERTS = 4
TOP = 2
STEP = 10
QW = 2048
CAP = 96
LANES = 128

NORM_EPS = 1e-05
ADAM_EPS = 1e-08
BETA_FIRST = 0.9
BETA_SECOND = 0.95
ROPE_BASE = 10000.0
MASK_FILL = -1000000000.0
SCALE = HD ** (-0.5)
HIGHEST = lax.Precision.HIGHEST
F32 = jnp.float32
BF16 = jnp.bfloat16


def matmul(left_side, right_side):
    return jnp.dot(left_side, right_side, preferred_element_type=F32)


def matmul_back(left_side, right_side):
    return lax.dot_general(
        left_side, right_side, (((1,), (1,)), ((), ())), preferred_element_type=F32
    )


def matmul_rows(left_side, right_side):
    return lax.dot_general(
        left_side, right_side, (((0,), (0,)), ((), ())), preferred_element_type=F32
    )


def exact_back(left_side, right_side):
    return lax.dot_general(
        left_side,
        right_side,
        (((1,), (1,)), ((), ())),
        precision=HIGHEST,
        preferred_element_type=F32,
    )


def exact_rows(left_side, right_side):
    return lax.dot_general(
        left_side,
        right_side,
        (((0,), (0,)), ((), ())),
        precision=HIGHEST,
        preferred_element_type=F32,
    )


def rope_tables(length):
    half_dim = HD // 2
    frequency = ROPE_BASE ** (-(2.0 * jnp.arange(half_dim, dtype=F32)) / HD)
    angles = jnp.arange(length, dtype=F32)[:, None] * frequency[None, :]
    cosine, sine = jnp.cos(angles), jnp.sin(angles)
    return (
        jnp.concatenate([cosine, cosine], axis=1),
        jnp.concatenate([-sine, sine], axis=1),
    )


def swap_perm(count, bits):
    return [(place, place ^ bits) for place in range(count)]


def core_swap(value):
    return lax.ppermute(value, "dp", swap_perm(lax.axis_size("dp"), 1))


def over_expert(value, bits):
    if bits == 0:
        return value
    return lax.ppermute(value, "expert", swap_perm(lax.axis_size("expert"), bits))


def chip_groups():
    count = lax.axis_size("dp")
    return [[2 * place + core for place in range(count // 2)] for core in range(2)]


def gather_chips(block):
    return lax.all_gather(block, "dp", axis=0, tiled=True, axis_index_groups=chip_groups())


def scatter_chips(partial):
    return lax.psum_scatter(
        partial, "dp", scatter_dimension=0, tiled=True, axis_index_groups=chip_groups()
    )


def in_core_order(core, mine, other, axis):
    return jnp.where(
        core == 0,
        jnp.concatenate([mine, other], axis=axis),
        jnp.concatenate([other, mine], axis=axis),
    )


def halves_of(core, whole):
    width = whole.shape[-1] // 2
    return tuple(
        lax.dynamic_slice_in_dim(whole, at * width, width, whole.ndim - 1) for at in (core, 1 - core)
    )


def fill(shape, parts):
    buffer = jnp.zeros(shape, BF16)
    for part, row, column in parts:
        buffer = lax.dynamic_update_slice(buffer, part, (row, column))
    return buffer


def exchange_rows(core, summed):
    rows = summed.shape[0] // 2
    low, high = summed[:rows], summed[rows:]
    mine = jnp.where(core == 0, low, high)
    return (mine, core_swap(jnp.where(core == 0, high, low)))


def slots_before(hits):
    count = hits.shape[-2]
    place = jnp.arange(count, dtype=jnp.int32)
    earlier = (place[:, None] > place[None, :]).astype(BF16)
    return jnp.einsum(
        "ts,...sn->...tn", earlier, hits.astype(BF16), preferred_element_type=F32
    ).astype(jnp.int32)


def route_tables(routes, names):
    hit = routes[:, :, None] == names[None, None, :]
    named = jnp.any(hit, axis=1)
    slot = slots_before(named)
    at_slot = slot[:, :, None] == jnp.arange(CAP, dtype=jnp.int32)[None, None, :]
    pick = (named[:, :, None] & at_slot).astype(BF16).transpose(1, 2, 0)
    back = (hit[:, :, :, None] & at_slot[:, None]).astype(BF16)
    back = back.transpose(1, 0, 2, 3).reshape(TOP, routes.shape[0], -1)
    return (pick, back, hit.astype(F32))


def chosen_gates(logits, routes):
    hit = routes[:, :, None] == jnp.arange(EXPERTS, dtype=jnp.int32)[None, None, :]
    picked = jnp.sum(jnp.where(hit, logits[:, None, :], 0.0), axis=2)
    return jax.nn.softmax(picked, axis=-1)


def gate_back(gates, grad_gates, routes):
    hit = routes[:, :, None] == jnp.arange(EXPERTS, dtype=jnp.int32)[None, None, :]
    centred = gates * (grad_gates - jnp.sum(gates * grad_gates, axis=-1, keepdims=True))
    return jnp.sum(centred[:, :, None] * hit.astype(F32), axis=1)


def norm_back(values, inverse, gain_row, grad_normed):
    scaled = gain_row * grad_normed
    grad_values = inverse * scaled - values * inverse**3 * jnp.mean(
        scaled * values, axis=-1, keepdims=True
    )
    grad_gain = jnp.sum(grad_normed * values * inverse, axis=0)
    return (grad_values, grad_gain)


def place_rows(blocks, places):
    rows, width = blocks[0].shape
    got = jnp.zeros((len(blocks) * rows, width), blocks[0].dtype)
    for block, place in zip(blocks, places):
        got = lax.dynamic_update_slice_in_dim(got, block, place * rows, 0)
    return jnp.concatenate([got, core_swap(got)])


def send_rows(blocks, places=None):
    blocks = [over_expert(block, bits) for bits, block in enumerate(blocks)]
    return place_rows(blocks, range(len(blocks)) if places is None else places)


def return_rows(partial, partners, places=None, between=()):
    count = partial.shape[0] // 2
    got = core_swap(partial[count:].astype(BF16))
    summed = (partial[:count] + got.astype(F32)).astype(BF16)
    rows = count // partners
    places = range(partners) if places is None else places
    blocks = [lax.dynamic_slice_in_dim(summed, place * rows, rows, 0) for place in places]
    blocks[-1] = after(blocks[-1], *between)
    return [over_expert(block, bits) for bits, block in enumerate(blocks)]


def over_chips(value, bits):
    if bits == 0:
        return value
    return lax.ppermute(value, "dp", swap_perm(lax.axis_size("dp"), 2 * bits))


def gather_small(chip, block):
    count, rows = lax.axis_size("dp") // 2, block.shape[0]
    whole = jnp.zeros((count * rows, block.shape[1]), block.dtype)
    for bits in range(count):
        whole = lax.dynamic_update_slice_in_dim(
            whole, over_chips(block, bits), (chip ^ bits) * rows, 0
        )
    return whole


def rotate(value, cosine, sine):
    half_dim = HD // 2
    swapped = jnp.concatenate([value[..., half_dim:], value[..., :half_dim]], axis=-1)
    return value * cosine + swapped * sine


def by_heads(rows, sequences):
    heads = rows.shape[1] // HD
    return rows.reshape(-1, heads, HD).transpose(1, 0, 2).reshape(heads, sequences, -1, HD)


def from_heads(blocks):
    heads = blocks.shape[0]
    return blocks.reshape(heads, -1, HD).transpose(1, 0, 2).reshape(-1, heads * HD)


def heads_dot(left_side, right_side, left_axis, right_axis):
    return lax.dot_general(
        left_side,
        right_side,
        (((left_axis,), (right_axis,)), ((0, 1), (0, 1))),
        preferred_element_type=F32,
    )


def turned(rows):
    return with_layout_constraint(rows.T.astype(F32), Layout(major_to_minor=(0, 1)))


def all_sum(value):
    bits = 1
    while bits < lax.axis_size("dp"):
        value = value + lax.ppermute(value, "dp", swap_perm(lax.axis_size("dp"), bits))
        bits *= 2
    bits = 1
    while bits < lax.axis_size("expert"):
        value = value + over_expert(value, bits)
        bits *= 2
    return value


def after(value, *others):
    return lax.optimization_barrier((value, *others))[0]


def together(*groups):
    return lax.optimization_barrier(groups)


def adam_step(moment, square, gradient):
    moment_new = BETA_FIRST * moment + (1.0 - BETA_FIRST) * gradient
    square_new = BETA_SECOND * square + (1.0 - BETA_SECOND) * gradient * gradient
    moment_hat = moment_new / (1.0 - BETA_FIRST**STEP)
    square_hat = square_new / (1.0 - BETA_SECOND**STEP)
    direction = moment_hat / (jnp.sqrt(square_hat) + ADAM_EPS)
    return (gradient, direction, moment_new, square_new)


def body(
    tokens,
    teacher,
    attn_routes,
    mlp_routes,
    image_mask,
    valid,
    master_query,
    moment_query,
    square_query,
    master_project,
    moment_project,
    square_project,
    master_gate_up,
    moment_gate_up,
    square_gate_up,
    master_down,
    moment_down,
    square_down,
    master_key_value,
    moment_key_value,
    square_key_value,
    master_router,
    moment_router,
    square_router,
    master_gains,
    moment_gains,
    square_gains,
):
    partners = lax.axis_size("expert")
    halves = partners // EXPERTS
    core, chip = lax.axis_index("dp") % 2, lax.axis_index("dp") // 2
    expert_at = lax.axis_index("expert")
    expert, half = expert_at // halves, expert_at % halves
    names = (expert_at ^ jnp.arange(partners, dtype=jnp.int32)) // halves
    token_count = tokens.shape[0]
    sequences = 2 * partners
    sixth = master_query.shape[1] // (2 * EXPERTS)

    valid_f = valid.astype(F32)
    marks = jnp.concatenate([attn_routes, image_mask[:, None]], axis=1).astype(BF16)
    marks = jnp.pad(marks, ((0, 0), (0, LANES - marks.shape[1])))
    payload = jnp.concatenate([tokens, marks], axis=1)
    places = [expert_at ^ bits for bits in range(partners)]

    map_rows = master_query.shape[0]
    row_mine, row_got = core * map_rows, (1 - core) * map_rows
    query_mine, query_theirs = halves_of(core, master_query)
    project_mine, project_theirs = halves_of(core, master_project.astype(BF16).T)
    width_attn = query_mine.shape[1]
    attn_rows = fill(
        (2 * map_rows, 2 * width_attn),
        [
            (query_mine.astype(BF16), row_mine, 0),
            (project_mine, row_mine, width_attn),
            (core_swap(query_theirs.astype(BF16)), row_got, 0),
            (core_swap(project_theirs), row_got, width_attn),
        ],
    )
    weight_attn = gather_chips(attn_rows)
    weight_query, weight_project = weight_attn[:, :width_attn], weight_attn[:, width_attn:]

    local_rows = master_key_value.shape[0]
    small = jnp.concatenate(
        [
            master_router,
            master_gains.T,
            jnp.full((local_rows, 1), jnp.sum(valid_f)),
        ],
        axis=1,
    ).astype(BF16)
    small = jnp.pad(small, ((0, 0), (0, LANES - small.shape[1])))
    half_width = EXPERTS * sixth

    def for_core(at):
        return jnp.concatenate(
            [
                lax.dynamic_slice_in_dim(
                    master_key_value, side * QW + (2 * part + at) * half_width, half_width, 1
                )
                for side in range(2)
                for part in range(halves)
            ],
            axis=1,
        ).astype(BF16)

    kv_mine = jnp.concatenate([for_core(core), small], axis=1)
    kv_got = core_swap(jnp.concatenate([for_core(1 - core), small], axis=1))

    def block_for(rows, bits):
        other = expert_at ^ bits
        column = ((other % halves) * EXPERTS + other // halves) * sixth
        return jnp.concatenate(
            [
                lax.dynamic_slice_in_dim(rows, column, sixth, 1),
                lax.dynamic_slice_in_dim(rows, halves * half_width + column, sixth, 1),
                rows[:, 2 * halves * half_width :],
            ],
            axis=1,
        )

    kv_pair = in_core_order(core, kv_mine, kv_got, 0)
    kv_blocks = [block_for(kv_pair, bits) for bits in range(partners)]

    width_ff = master_gate_up.shape[2] // 2
    kv_blocks = [over_expert(block, bits) for bits, block in enumerate(kv_blocks)]
    kv_blocks, payload = together(kv_blocks, payload)
    token_blocks = [over_expert(payload, bits) for bits in range(partners)]
    arrived = jnp.zeros((2 * partners * local_rows, 2 * sixth + LANES), BF16)
    for block, at in zip(kv_blocks, places):
        arrived = lax.dynamic_update_slice_in_dim(arrived, block, at * 2 * local_rows, 0)
    arrived = arrived.reshape(partners, 2, local_rows, -1).transpose(1, 0, 2, 3)
    arrived = arrived.reshape(2 * partners * local_rows, -1)
    arrived, master_gate_up, _ = together(arrived, master_gate_up, attn_rows)
    gate_mine, gate_theirs = halves_of(core, master_gate_up[0])
    up_mine, up_theirs = halves_of(core, master_gate_up[1])
    gate_up_rows = fill(
        (2 * map_rows, 2 * width_ff),
        [
            (gate_mine.astype(BF16), row_mine, 0),
            (up_mine.astype(BF16), row_mine, width_ff),
            (core_swap(gate_theirs.astype(BF16)), row_got, 0),
            (core_swap(up_theirs.astype(BF16)), row_got, width_ff),
        ],
    )
    shared_whole = gather_small(chip, arrived)
    shared_whole, token_blocks, _ = together(shared_whole, token_blocks, gate_up_rows)
    everyone = place_rows(token_blocks, places)
    kv_weight = shared_whole[:, : 2 * sixth]
    small_whole = shared_whole[:, 2 * sixth :]
    router_low = small_whole[:, : 2 * EXPERTS]
    router_f = router_low.astype(F32)
    gains_f = small_whole[:, 2 * EXPERTS : 2 * EXPERTS + 2].astype(F32).T
    total_count = jnp.sum(small_whole[:, 2 * EXPERTS + 2].astype(F32)) / local_rows

    weight_gate_up = gather_chips(gate_up_rows)
    down_mine, down_theirs = halves_of(core, master_down.astype(BF16).T)
    down_rows = fill(
        (2 * map_rows, width_ff),
        [(down_mine, row_mine, 0), (core_swap(down_theirs), row_got, 0)],
    )
    weight_down = gather_chips(down_rows)

    tables = rope_tables(token_count)
    inputs_all = everyone[:, :D].astype(F32)
    inverse_all = lax.rsqrt(jnp.mean(inputs_all * inputs_all, axis=-1, keepdims=True) + NORM_EPS)
    normed_all = (inputs_all * inverse_all * gains_f[0]).astype(BF16)
    inputs_f = tokens.astype(F32)
    inverse_one, normed_one = (
        lax.dynamic_slice_in_dim(table, expert_at * token_count, token_count, 0)
        for table in (inverse_all, normed_all)
    )
    marks_all = everyone[:, D:].astype(F32).reshape(sequences, token_count, LANES)
    named_all = jnp.any(marks_all[:, :, :TOP] == expert.astype(F32), axis=2)
    slot_all = slots_before(named_all[:, :, None])[:, :, 0]
    slots = jnp.arange(CAP, dtype=jnp.int32)
    pick_all = (named_all[:, None, :] & (slot_all[:, None, :] == slots[None, :, None])).astype(BF16)
    image_on = marks_all[:, :, TOP] > 0.0
    position = jnp.arange(token_count, dtype=jnp.int32)
    allowed = (position[:, None] >= position[None, :])[None] | (
        image_on[:, :, None] & image_on[:, None, :]
    )

    kv_heads = by_heads(matmul(normed_all, kv_weight), sequences)
    count = sixth // HD
    kv_own = jnp.concatenate(
        [rotate(kv_heads[:count], *tables).astype(BF16), kv_heads[count:].astype(BF16)]
    )
    query_pre = matmul(normed_all, weight_query)
    query_heads = rotate(by_heads(query_pre, sequences), *tables).astype(BF16)
    kv_shared = [over_expert(kv_own, step * halves) for step in range(EXPERTS - 1)]
    kv_shared.append(over_expert(after(kv_own, query_heads, down_rows), (EXPERTS - 1) * halves))

    def every_head(parts):
        whole = jnp.zeros((EXPERTS * count,) + parts[0].shape[1:], BF16)
        for step, part in enumerate(parts):
            whole = lax.dynamic_update_slice_in_dim(whole, part, (expert ^ step) * count, 0)
        return whole

    key_heads = every_head([part[:count] for part in kv_shared])
    value_heads = every_head([part[count:] for part in kv_shared])
    scores = heads_dot(query_heads, key_heads, 3, 3) * SCALE
    scores = jnp.where(allowed[None], scores, MASK_FILL)
    probs = jax.nn.softmax(scores, axis=-1)
    probs_low = probs.astype(BF16)
    attended_all = from_heads(heads_dot(probs_low, value_heads, 3, 2).astype(BF16))

    def per_sequence(table, rows, left_axis):
        blocks = rows.reshape(sequences, -1, rows.shape[1])
        picked = lax.dot_general(
            table, blocks, (((left_axis,), (1,)), ((0,), (0,))), preferred_element_type=F32
        )
        return picked.astype(BF16).reshape(-1, rows.shape[1])

    attended = per_sequence(pick_all, attended_all, 2)

    attn_pick, attn_back, attn_hit = route_tables(attn_routes, names)
    gates_attn = chosen_gates(matmul(normed_one, router_low[:, :EXPERTS]), attn_routes)
    branch_rows = jnp.concatenate(
        return_rows(matmul_back(attended, weight_project), partners, places)
    )
    branch = [matmul(attn_back[choice], branch_rows) for choice in range(TOP)]
    hidden = inputs_f + sum(gates_attn[:, choice, None] * branch[choice] for choice in range(TOP))

    inverse_two = lax.rsqrt(jnp.mean(hidden * hidden, axis=-1, keepdims=True) + NORM_EPS)
    normed_two = (hidden * inverse_two * gains_f[1]).astype(BF16)
    mlp_pick, mlp_back, mlp_hit = route_tables(mlp_routes, names)
    gates_mlp = chosen_gates(matmul(normed_two, router_low[:, EXPERTS:]), mlp_routes)
    placed = matmul(mlp_pick.reshape(-1, token_count), normed_two).astype(BF16)
    rows_two = send_rows(list(placed.reshape(partners, CAP, D)))
    gate_up_val = matmul(rows_two, weight_gate_up)
    gate_val, up_val = gate_up_val[:, :width_ff], gate_up_val[:, width_ff:]
    active = (jax.nn.silu(gate_val) * up_val).astype(BF16)
    mlp_rows = jnp.concatenate(return_rows(matmul_back(active, weight_down), partners))
    mlp_branch = [matmul(mlp_back[choice], mlp_rows) for choice in range(TOP)]
    outputs = hidden + sum(gates_mlp[:, choice, None] * mlp_branch[choice] for choice in range(TOP))

    deviation = outputs - teacher.astype(F32)
    local_error = jnp.sum(valid_f[:, None] * deviation * deviation)
    total_error = all_sum(local_error.reshape(1, 1))[0, 0]
    grad_out = 2.0 * valid_f[:, None] * deviation / total_count

    def send_grads(pick, gates, hit, grad, where=None):
        gate_of = jnp.sum(gates[:, :, None] * hit, axis=1)
        rows = (gate_of.T[:, :, None] * grad[None]).astype(BF16)
        sent = jnp.einsum("kct,ktd->kcd", pick, rows, preferred_element_type=F32).astype(BF16)
        return send_rows(list(sent), where)

    rows_grad = send_grads(mlp_pick, gates_mlp, mlp_hit, grad_out)
    grad_down = matmul_rows(rows_grad, active).astype(BF16)
    grad_active = matmul(rows_grad, weight_down)
    sigmoid_gate = jax.nn.sigmoid(gate_val)
    grad_gate = (
        grad_active * up_val * sigmoid_gate * (1.0 + gate_val * (1.0 - sigmoid_gate))
    ).astype(BF16)
    grad_up = (grad_active * gate_val * sigmoid_gate).astype(BF16)
    grad_both = jnp.concatenate([grad_gate, grad_up], axis=1)
    down_sum = scatter_chips(grad_down)
    grad_gate_up = matmul_rows(rows_two, grad_both).astype(BF16)
    normed_two_rows = return_rows(
        matmul_back(after(grad_both, grad_down), weight_gate_up), partners
    )
    gate_up_sum = scatter_chips(after(grad_gate_up, down_sum, *normed_two_rows))
    grad_gates_mlp = jnp.stack(
        [jnp.sum(grad_out * mlp_branch[choice], axis=-1) for choice in range(TOP)], axis=1
    )
    grad_logits_mlp = gate_back(gates_mlp, grad_gates_mlp, mlp_routes)
    grad_normed_two = matmul(
        jnp.sum(mlp_back, axis=0), jnp.concatenate(normed_two_rows)
    ) + exact_back(grad_logits_mlp, router_f[:, EXPERTS:])
    grad_hidden_norm, grad_gain_two = norm_back(hidden, inverse_two, gains_f[1], grad_normed_two)
    grad_hidden = grad_out + grad_hidden_norm
    grad_router_two = exact_rows(normed_two.astype(F32), grad_logits_mlp)

    rows_grad_attn = send_grads(attn_pick, gates_attn, attn_hit, grad_hidden, places)
    grad_project = matmul_rows(rows_grad_attn, attended).astype(BF16)
    grad_attended = matmul(rows_grad_attn, weight_project).astype(BF16)
    grad_gates_attn = jnp.stack(
        [jnp.sum(grad_hidden * branch[choice], axis=-1) for choice in range(TOP)], axis=1
    )
    grad_logits_attn = gate_back(gates_attn, grad_gates_attn, attn_routes)
    grad_heads = by_heads(per_sequence(pick_all, grad_attended, 1), sequences)
    grad_probs = heads_dot(grad_heads, value_heads, 3, 3)
    inner = jnp.sum(probs * grad_probs, axis=-1, keepdims=True)
    grad_scores = (probs * (grad_probs - inner)).astype(BF16)
    grad_query_heads = heads_dot(grad_scores, key_heads, 3, 2) * SCALE
    grad_key_heads = heads_dot(grad_scores, query_heads, 2, 2) * SCALE
    grad_value_heads = heads_dot(probs_low, grad_heads, 2, 2)
    back_tables = (tables[0], -tables[1])
    grad_query_pre = from_heads(rotate(grad_query_heads, *back_tables).astype(BF16))
    grad_keys = rotate(grad_key_heads, *back_tables).astype(BF16)
    grad_values = grad_value_heads.astype(BF16)
    grad_query = matmul_rows(normed_all, grad_query_pre).astype(BF16)
    down_mine, down_other = exchange_rows(core, down_sum)
    reduced_down = turned(in_core_order(core, down_mine, down_other, 1))
    update_down = adam_step(moment_down, square_down, reduced_down)

    def heads_of(step):
        start = (expert ^ step) * count
        return jnp.concatenate(
            [
                lax.dynamic_slice_in_dim(table, start, count, 0)
                for table in (grad_keys, grad_values)
            ]
        )

    grad_kv_parts = [heads_of(step) for step in range(EXPERTS)]
    grad_kv_parts[-1] = after(grad_kv_parts[-1], grad_query, total_error, *update_down)
    grad_kv = sum(
        over_expert(part, step * halves).astype(F32) for step, part in enumerate(grad_kv_parts)
    ).astype(BF16)
    grad_kv = from_heads(grad_kv)
    grad_kv_weight = matmul_rows(normed_all, grad_kv).astype(BF16)
    normed_one_partial = matmul_back(grad_query_pre, weight_query) + matmul_back(
        grad_kv, kv_weight
    )
    grad_normed_router = exact_back(grad_logits_attn, router_f[:, :EXPERTS])
    grad_gain_one = jnp.sum(normed_one_partial * inputs_all * inverse_all, axis=0) + jnp.sum(
        grad_normed_router * inputs_f * inverse_one, axis=0
    )
    grad_small = jnp.concatenate(
        [
            exact_rows(normed_one.astype(F32), grad_logits_attn),
            grad_router_two,
            grad_gain_one[:, None],
            grad_gain_two[:, None],
        ],
        axis=1,
    ).astype(BF16)
    grad_small = jnp.pad(grad_small, ((0, 0), (0, LANES - grad_small.shape[1])))
    last_rows = fill(
        (grad_query.shape[0], 2 * width_attn + 2 * sixth + LANES),
        [
            (grad_project, 0, width_attn),
            (grad_query, 0, 0),
            (grad_kv_weight, 0, 2 * width_attn),
            (grad_small, 0, 2 * width_attn + 2 * sixth),
        ],
    )
    last_sum = scatter_chips(after(last_rows, gate_up_sum))
    gate_up_mine, gate_up_other = exchange_rows(core, gate_up_sum)
    reduced_gate_up = jnp.stack(
        [
            in_core_order(
                core,
                gate_up_mine[:, at * width_ff : (at + 1) * width_ff],
                gate_up_other[:, at * width_ff : (at + 1) * width_ff],
                1,
            )
            for at in range(2)
        ]
    )
    reduced_gate_up = with_layout_constraint(
        reduced_gate_up, Layout(major_to_minor=(0, 1, 2))
    ).astype(F32)
    update_gate_up = adam_step(moment_gate_up, square_gate_up, reduced_gate_up)
    normed_one_rows = return_rows(
        after(normed_one_partial, last_rows), partners, places, update_gate_up
    )
    grad_normed_one = sum(rows.astype(F32) for rows in normed_one_rows) + grad_normed_router
    grad_inputs_norm, _ = norm_back(inputs_f, inverse_one, gains_f[0], grad_normed_one)
    input_grad = grad_hidden + grad_inputs_norm

    last_mine, last_other = exchange_rows(core, last_sum)
    attn_mine, attn_other = last_mine[:, : 2 * width_attn], last_other[:, : 2 * width_attn]
    shared_mine, shared_theirs = [
        rows[:, 2 * width_attn :].reshape(partners, local_rows, -1)
        for rows in (last_mine, last_other)
    ]
    shared_pair = jnp.where(
        core == 0, jnp.stack([shared_mine, shared_theirs]), jnp.stack([shared_theirs, shared_mine])
    )
    received = jnp.stack(
        [
            over_expert(lax.dynamic_index_in_dim(shared_pair, expert_at ^ bits, 1, keepdims=False), bits)
            for bits in range(partners)
        ]
    )
    query_mine, project_mine = attn_mine[:, :width_attn], attn_mine[:, width_attn:]
    query_other, project_other = attn_other[:, :width_attn], attn_other[:, width_attn:]
    small_sum = jnp.sum(received[..., -LANES:].astype(F32), axis=(0, 1))
    received = jnp.stack(
        [lax.dynamic_index_in_dim(received, expert_at ^ at, 0, keepdims=False) for at in range(partners)]
    )
    reduced_kv = (
        received[..., :-LANES]
        .reshape(EXPERTS, halves, 2, local_rows, 2, sixth)
        .transpose(3, 4, 1, 2, 0, 5)
        .reshape(local_rows, -1)
        .astype(F32)
    )
    reduced_router = small_sum[:, : 2 * EXPERTS]
    reduced_gains = small_sum[:, 2 * EXPERTS : 2 * EXPERTS + 2].T
    reduced_query = with_layout_constraint(
        in_core_order(core, query_mine, query_other, 1), Layout(major_to_minor=(0, 1))
    ).astype(F32)
    reduced_project = turned(in_core_order(core, project_mine, project_other, 1))
    loss_value = total_error / total_count
    return (
        outputs,
        loss_value,
        input_grad,
        *adam_step(moment_query, square_query, reduced_query),
        *adam_step(moment_project, square_project, reduced_project),
        *update_gate_up,
        *update_down,
        *adam_step(moment_key_value, square_key_value, reduced_kv),
        *adam_step(moment_router, square_router, reduced_router),
        *adam_step(moment_gains, square_gains, reduced_gains),
    )


def solution(mesh):
    rows = P(("dp", "expert"), None)
    flat = P(("dp", "expert"))
    columns = P(None, ("dp", "expert"))
    query, project, gate_up = P("dp", "expert"), P("expert", "dp"), P(None, "dp", "expert")
    weights = (query, project, gate_up, project, rows, rows, columns)
    return jax.shard_map(
        body,
        mesh=mesh,
        in_specs=(rows, rows, rows, rows, flat, flat)
        + tuple(spec for spec in weights for _ in range(3)),
        out_specs=(rows, P(), rows) + tuple(spec for spec in weights for _ in range(4)),
        check_vma=False,
    )
```

```python
import jax
import jax.numpy as jnp
from jax import lax
from jax.experimental.layout import Layout, with_layout_constraint
from jax.sharding import PartitionSpec as P

D = 2048
HD = 128
EXPERTS = 4
TOP = 2
STEP = 10
QW = 2048
CAP = 96
LANES = 128

NORM_EPS = 1e-05
ADAM_EPS = 1e-08
BETA_FIRST = 0.9
BETA_SECOND = 0.95
ROPE_BASE = 10000.0
MASK_FILL = -1000000000.0
SCALE = HD ** (-0.5)
HIGHEST = lax.Precision.HIGHEST
F32 = jnp.float32
BF16 = jnp.bfloat16


def matmul(left_side, right_side):
    return jnp.dot(left_side, right_side, preferred_element_type=F32)


def matmul_back(left_side, right_side):
    return lax.dot_general(
        left_side, right_side, (((1,), (1,)), ((), ())), preferred_element_type=F32
    )


def matmul_rows(left_side, right_side):
    return lax.dot_general(
        left_side, right_side, (((0,), (0,)), ((), ())), preferred_element_type=F32
    )


def exact_back(left_side, right_side):
    return lax.dot_general(
        left_side,
        right_side,
        (((1,), (1,)), ((), ())),
        precision=HIGHEST,
        preferred_element_type=F32,
    )


def exact_rows(left_side, right_side):
    return lax.dot_general(
        left_side,
        right_side,
        (((0,), (0,)), ((), ())),
        precision=HIGHEST,
        preferred_element_type=F32,
    )


def rope_tables(length):
    half_dim = HD // 2
    frequency = ROPE_BASE ** (-(2.0 * jnp.arange(half_dim, dtype=F32)) / HD)
    angles = jnp.arange(length, dtype=F32)[:, None] * frequency[None, :]
    cosine, sine = jnp.cos(angles), jnp.sin(angles)
    return (
        jnp.concatenate([cosine, cosine], axis=1),
        jnp.concatenate([-sine, sine], axis=1),
    )


def swap_perm(count, bits):
    return [(place, place ^ bits) for place in range(count)]


def core_swap(value):
    return lax.ppermute(value, "dp", swap_perm(lax.axis_size("dp"), 1))


def over_expert(value, bits):
    if bits == 0:
        return value
    return lax.ppermute(value, "expert", swap_perm(lax.axis_size("expert"), bits))


def chip_groups():
    count = lax.axis_size("dp")
    return [[2 * place + core for place in range(count // 2)] for core in range(2)]


def gather_chips(block):
    return lax.all_gather(block, "dp", axis=0, tiled=True, axis_index_groups=chip_groups())


def scatter_chips(partial):
    return lax.psum_scatter(
        partial, "dp", scatter_dimension=0, tiled=True, axis_index_groups=chip_groups()
    )


def in_core_order(core, mine, other, axis):
    return jnp.where(
        core == 0,
        jnp.concatenate([mine, other], axis=axis),
        jnp.concatenate([other, mine], axis=axis),
    )


def halves_of(core, whole):
    width = whole.shape[-1] // 2
    return tuple(
        lax.dynamic_slice_in_dim(whole, at * width, width, whole.ndim - 1) for at in (core, 1 - core)
    )


def fill(shape, parts):
    buffer = jnp.zeros(shape, BF16)
    for part, row, column in parts:
        buffer = lax.dynamic_update_slice(buffer, part, (row, column))
    return buffer


def exchange_rows(core, summed):
    rows = summed.shape[0] // 2
    mine, theirs = [
        lax.dynamic_slice_in_dim(summed, at * rows, rows, 0) for at in (core, 1 - core)
    ]
    return (mine, core_swap(theirs))


def slots_before(hits):
    count = hits.shape[-2]
    place = jnp.arange(count, dtype=jnp.int32)
    earlier = (place[:, None] > place[None, :]).astype(BF16)
    return jnp.einsum(
        "ts,...sn->...tn", earlier, hits.astype(BF16), preferred_element_type=F32
    ).astype(jnp.int32)


def route_tables(routes, names):
    hit = routes[:, :, None] == names[None, None, :]
    named = jnp.any(hit, axis=1)
    slot = slots_before(named)
    at_slot = slot[:, :, None] == jnp.arange(CAP, dtype=jnp.int32)[None, None, :]
    pick = (named[:, :, None] & at_slot).astype(BF16).transpose(1, 2, 0)
    back = (hit[:, :, :, None] & at_slot[:, None]).astype(BF16)
    back = back.transpose(1, 0, 2, 3).reshape(TOP, routes.shape[0], -1)
    return (pick, back, hit.astype(F32))


def chosen_gates(logits, routes):
    hit = routes[:, :, None] == jnp.arange(EXPERTS, dtype=jnp.int32)[None, None, :]
    picked = jnp.sum(jnp.where(hit, logits[:, None, :], 0.0), axis=2)
    return jax.nn.softmax(picked, axis=-1)


def gate_back(gates, grad_gates, routes):
    hit = routes[:, :, None] == jnp.arange(EXPERTS, dtype=jnp.int32)[None, None, :]
    centred = gates * (grad_gates - jnp.sum(gates * grad_gates, axis=-1, keepdims=True))
    return jnp.sum(centred[:, :, None] * hit.astype(F32), axis=1)


def norm_back(values, inverse, gain_row, grad_normed):
    scaled = gain_row * grad_normed
    grad_values = inverse * scaled - values * inverse**3 * jnp.mean(
        scaled * values, axis=-1, keepdims=True
    )
    grad_gain = jnp.sum(grad_normed * values * inverse, axis=0)
    return (grad_values, grad_gain)


def place_rows(blocks, places):
    rows, width = blocks[0].shape
    got = jnp.zeros((len(blocks) * rows, width), blocks[0].dtype)
    for block, place in zip(blocks, places):
        got = lax.dynamic_update_slice_in_dim(got, block, place * rows, 0)
    return jnp.concatenate([got, core_swap(got)])


def send_rows(blocks, places=None):
    blocks = [over_expert(block, bits) for bits, block in enumerate(blocks)]
    return place_rows(blocks, range(len(blocks)) if places is None else places)


def return_rows(partial, partners, places=None, between=()):
    count = partial.shape[0] // 2
    got = core_swap(partial[count:].astype(BF16))
    summed = (partial[:count] + got.astype(F32)).astype(BF16)
    rows = count // partners
    places = range(partners) if places is None else places
    blocks = [lax.dynamic_slice_in_dim(summed, place * rows, rows, 0) for place in places]
    blocks[-1] = after(blocks[-1], *between)
    return [over_expert(block, bits) for bits, block in enumerate(blocks)]


def over_chips(value, bits):
    if bits == 0:
        return value
    return lax.ppermute(value, "dp", swap_perm(lax.axis_size("dp"), 2 * bits))


def gather_small(chip, block):
    count, rows = lax.axis_size("dp") // 2, block.shape[0]
    whole = jnp.zeros((count * rows, block.shape[1]), block.dtype)
    for bits in range(count):
        whole = lax.dynamic_update_slice_in_dim(
            whole, over_chips(block, bits), (chip ^ bits) * rows, 0
        )
    return whole


def rotate(value, cosine, sine):
    half_dim = HD // 2
    swapped = jnp.concatenate([value[..., half_dim:], value[..., :half_dim]], axis=-1)
    return value * cosine + swapped * sine


def by_heads(rows, sequences):
    heads = rows.shape[1] // HD
    return rows.reshape(-1, heads, HD).transpose(1, 0, 2).reshape(heads, sequences, -1, HD)


def from_heads(blocks):
    heads = blocks.shape[0]
    return blocks.reshape(heads, -1, HD).transpose(1, 0, 2).reshape(-1, heads * HD)


def heads_dot(left_side, right_side, left_axis, right_axis):
    return lax.dot_general(
        left_side,
        right_side,
        (((left_axis,), (right_axis,)), ((0, 1), (0, 1))),
        preferred_element_type=F32,
    )


def turned(rows):
    return with_layout_constraint(rows.T.astype(F32), Layout(major_to_minor=(0, 1)))


def all_sum(value):
    bits = 1
    while bits < lax.axis_size("dp"):
        value = value + lax.ppermute(value, "dp", swap_perm(lax.axis_size("dp"), bits))
        bits *= 2
    bits = 1
    while bits < lax.axis_size("expert"):
        value = value + over_expert(value, bits)
        bits *= 2
    return value


def after(value, *others):
    return lax.optimization_barrier((value, *others))[0]


def together(*groups):
    return lax.optimization_barrier(groups)


def adam_step(moment, square, gradient):
    moment_new = BETA_FIRST * moment + (1.0 - BETA_FIRST) * gradient
    square_new = BETA_SECOND * square + (1.0 - BETA_SECOND) * gradient * gradient
    moment_hat = moment_new / (1.0 - BETA_FIRST**STEP)
    square_hat = square_new / (1.0 - BETA_SECOND**STEP)
    direction = moment_hat / (jnp.sqrt(square_hat) + ADAM_EPS)
    return (gradient, direction, moment_new, square_new)


def body(
    tokens,
    teacher,
    attn_routes,
    mlp_routes,
    image_mask,
    valid,
    master_query,
    moment_query,
    square_query,
    master_project,
    moment_project,
    square_project,
    master_gate_up,
    moment_gate_up,
    square_gate_up,
    master_down,
    moment_down,
    square_down,
    master_key_value,
    moment_key_value,
    square_key_value,
    master_router,
    moment_router,
    square_router,
    master_gains,
    moment_gains,
    square_gains,
):
    partners = lax.axis_size("expert")
    halves = partners // EXPERTS
    core, chip = lax.axis_index("dp") % 2, lax.axis_index("dp") // 2
    expert_at = lax.axis_index("expert")
    expert, half = expert_at // halves, expert_at % halves
    names = (expert_at ^ jnp.arange(partners, dtype=jnp.int32)) // halves
    token_count = tokens.shape[0]
    sequences = 2 * partners
    sixth = master_query.shape[1] // (2 * EXPERTS)

    valid_f = valid.astype(F32)
    marks = jnp.concatenate([attn_routes, image_mask[:, None]], axis=1).astype(BF16)
    marks = jnp.pad(marks, ((0, 0), (0, LANES - marks.shape[1])))
    payload = jnp.concatenate([tokens, marks], axis=1)
    places = [expert_at ^ bits for bits in range(partners)]

    map_rows = master_query.shape[0]
    row_mine, row_got = core * map_rows, (1 - core) * map_rows
    query_mine, query_theirs = halves_of(core, master_query)
    project_mine, project_theirs = halves_of(core, master_project.astype(BF16).T)
    width_attn = query_mine.shape[1]
    attn_rows = fill(
        (2 * map_rows, 2 * width_attn),
        [
            (query_mine.astype(BF16), row_mine, 0),
            (project_mine, row_mine, width_attn),
            (core_swap(query_theirs.astype(BF16)), row_got, 0),
            (core_swap(project_theirs), row_got, width_attn),
        ],
    )
    weight_attn = gather_chips(attn_rows)
    weight_query, weight_project = weight_attn[:, :width_attn], weight_attn[:, width_attn:]

    local_rows = master_key_value.shape[0]
    small = jnp.concatenate(
        [
            master_router,
            master_gains.T,
            jnp.full((local_rows, 1), jnp.sum(valid_f)),
        ],
        axis=1,
    ).astype(BF16)
    small = jnp.pad(small, ((0, 0), (0, LANES - small.shape[1])))
    half_width = EXPERTS * sixth

    def for_core(at):
        return jnp.concatenate(
            [
                lax.dynamic_slice_in_dim(
                    master_key_value, side * QW + (2 * part + at) * half_width, half_width, 1
                )
                for side in range(2)
                for part in range(halves)
            ],
            axis=1,
        ).astype(BF16)

    kv_mine = jnp.concatenate([for_core(core), small], axis=1)
    kv_got = core_swap(jnp.concatenate([for_core(1 - core), small], axis=1))

    def block_for(rows, bits):
        other = expert_at ^ bits
        column = ((other % halves) * EXPERTS + other // halves) * sixth
        return jnp.concatenate(
            [
                lax.dynamic_slice_in_dim(rows, column, sixth, 1),
                lax.dynamic_slice_in_dim(rows, halves * half_width + column, sixth, 1),
                rows[:, 2 * halves * half_width :],
            ],
            axis=1,
        )

    kv_pair = in_core_order(core, kv_mine, kv_got, 0)
    kv_blocks = [block_for(kv_pair, bits) for bits in range(partners)]

    width_ff = master_gate_up.shape[2] // 2
    kv_blocks = [over_expert(block, bits) for bits, block in enumerate(kv_blocks)]
    kv_blocks, payload = together(kv_blocks, payload)
    token_blocks = [over_expert(payload, bits) for bits in range(partners)]
    arrived = jnp.zeros((2 * partners * local_rows, 2 * sixth + LANES), BF16)
    for block, at in zip(kv_blocks, places):
        arrived = lax.dynamic_update_slice_in_dim(arrived, block, at * 2 * local_rows, 0)
    arrived = arrived.reshape(partners, 2, local_rows, -1).transpose(1, 0, 2, 3)
    arrived = arrived.reshape(2 * partners * local_rows, -1)
    arrived, master_gate_up, _ = together(arrived, master_gate_up, attn_rows)
    gate_mine, gate_theirs = halves_of(core, master_gate_up[0])
    up_mine, up_theirs = halves_of(core, master_gate_up[1])
    gate_up_rows = fill(
        (2 * map_rows, 2 * width_ff),
        [
            (gate_mine.astype(BF16), row_mine, 0),
            (up_mine.astype(BF16), row_mine, width_ff),
            (core_swap(gate_theirs.astype(BF16)), row_got, 0),
            (core_swap(up_theirs.astype(BF16)), row_got, width_ff),
        ],
    )
    shared_whole = gather_small(chip, arrived)
    shared_whole, token_blocks, _ = together(shared_whole, token_blocks, gate_up_rows)
    everyone = place_rows(token_blocks, places)
    kv_weight = shared_whole[:, : 2 * sixth]
    small_whole = shared_whole[:, 2 * sixth :]
    router_low = small_whole[:, : 2 * EXPERTS]
    router_f = router_low.astype(F32)
    gains_f = small_whole[:, 2 * EXPERTS : 2 * EXPERTS + 2].astype(F32).T
    total_count = jnp.sum(small_whole[:, 2 * EXPERTS + 2].astype(F32)) / local_rows

    weight_gate_up = gather_chips(gate_up_rows)
    down_mine, down_theirs = halves_of(core, master_down.astype(BF16).T)
    down_rows = fill(
        (2 * map_rows, width_ff),
        [(down_mine, row_mine, 0), (core_swap(down_theirs), row_got, 0)],
    )
    weight_down = gather_chips(down_rows)

    tables = rope_tables(token_count)
    inputs_all = everyone[:, :D].astype(F32)
    inverse_all = lax.rsqrt(jnp.mean(inputs_all * inputs_all, axis=-1, keepdims=True) + NORM_EPS)
    normed_all = (inputs_all * inverse_all * gains_f[0]).astype(BF16)
    inputs_f = tokens.astype(F32)
    inverse_one, normed_one = (
        lax.dynamic_slice_in_dim(table, expert_at * token_count, token_count, 0)
        for table in (inverse_all, normed_all)
    )
    marks_all = everyone[:, D:].astype(F32).reshape(sequences, token_count, LANES)
    named_all = jnp.any(marks_all[:, :, :TOP] == expert.astype(F32), axis=2)
    slot_all = slots_before(named_all[:, :, None])[:, :, 0]
    slots = jnp.arange(CAP, dtype=jnp.int32)
    pick_all = (named_all[:, None, :] & (slot_all[:, None, :] == slots[None, :, None])).astype(BF16)
    image_on = marks_all[:, :, TOP] > 0.0
    position = jnp.arange(token_count, dtype=jnp.int32)
    allowed = (position[:, None] >= position[None, :])[None] | (
        image_on[:, :, None] & image_on[:, None, :]
    )

    kv_heads = by_heads(matmul(normed_all, kv_weight), sequences)
    count = sixth // HD
    kv_own = jnp.concatenate(
        [rotate(kv_heads[:count], *tables).astype(BF16), kv_heads[count:].astype(BF16)]
    )
    query_pre = matmul(normed_all, weight_query)
    query_heads = rotate(by_heads(query_pre, sequences), *tables).astype(BF16)
    kv_shared = [over_expert(kv_own, step * halves) for step in range(EXPERTS - 1)]
    kv_shared.append(over_expert(after(kv_own, query_heads, down_rows), (EXPERTS - 1) * halves))

    def every_head(parts):
        whole = jnp.zeros((EXPERTS * count,) + parts[0].shape[1:], BF16)
        for step, part in enumerate(parts):
            whole = lax.dynamic_update_slice_in_dim(whole, part, (expert ^ step) * count, 0)
        return whole

    key_heads = every_head([part[:count] for part in kv_shared])
    value_heads = every_head([part[count:] for part in kv_shared])
    scores = heads_dot(query_heads, key_heads, 3, 3) * SCALE
    scores = jnp.where(allowed[None], scores, MASK_FILL)
    probs = jax.nn.softmax(scores, axis=-1)
    probs_low = probs.astype(BF16)
    attended_all = from_heads(heads_dot(probs_low, value_heads, 3, 2).astype(BF16))

    def per_sequence(table, rows, left_axis):
        blocks = rows.reshape(sequences, -1, rows.shape[1])
        picked = lax.dot_general(
            table, blocks, (((left_axis,), (1,)), ((0,), (0,))), preferred_element_type=F32
        )
        return picked.astype(BF16).reshape(-1, rows.shape[1])

    attended = per_sequence(pick_all, attended_all, 2)

    attn_pick, attn_back, attn_hit = route_tables(attn_routes, names)
    gates_attn = chosen_gates(matmul(normed_one, router_low[:, :EXPERTS]), attn_routes)
    branch_rows = jnp.concatenate(
        return_rows(matmul_back(attended, weight_project), partners, places)
    )
    branch = [matmul(attn_back[choice], branch_rows) for choice in range(TOP)]
    hidden = inputs_f + sum(gates_attn[:, choice, None] * branch[choice] for choice in range(TOP))

    inverse_two = lax.rsqrt(jnp.mean(hidden * hidden, axis=-1, keepdims=True) + NORM_EPS)
    normed_two = (hidden * inverse_two * gains_f[1]).astype(BF16)
    mlp_pick, mlp_back, mlp_hit = route_tables(mlp_routes, names)
    gates_mlp = chosen_gates(matmul(normed_two, router_low[:, EXPERTS:]), mlp_routes)
    placed = matmul(mlp_pick.reshape(-1, token_count), normed_two).astype(BF16)
    rows_two = send_rows(list(placed.reshape(partners, CAP, D)))
    gate_up_val = matmul(rows_two, weight_gate_up)
    gate_val, up_val = gate_up_val[:, :width_ff], gate_up_val[:, width_ff:]
    active = (jax.nn.silu(gate_val) * up_val).astype(BF16)
    mlp_rows = jnp.concatenate(return_rows(matmul_back(active, weight_down), partners))
    mlp_branch = [matmul(mlp_back[choice], mlp_rows) for choice in range(TOP)]
    outputs = hidden + sum(gates_mlp[:, choice, None] * mlp_branch[choice] for choice in range(TOP))

    deviation = outputs - teacher.astype(F32)
    local_error = jnp.sum(valid_f[:, None] * deviation * deviation)
    grad_out = 2.0 * valid_f[:, None] * deviation / total_count

    def send_grads(pick, gates, hit, grad, where=None):
        gate_of = jnp.sum(gates[:, :, None] * hit, axis=1)
        rows = (gate_of.T[:, :, None] * grad[None]).astype(BF16)
        sent = jnp.einsum("kct,ktd->kcd", pick, rows, preferred_element_type=F32).astype(BF16)
        return send_rows(list(sent), where)

    rows_grad = send_grads(mlp_pick, gates_mlp, mlp_hit, grad_out)
    grad_down = matmul_rows(rows_grad, active).astype(BF16)
    grad_active = matmul(rows_grad, weight_down)
    sigmoid_gate = jax.nn.sigmoid(gate_val)
    grad_gate = (
        grad_active * up_val * sigmoid_gate * (1.0 + gate_val * (1.0 - sigmoid_gate))
    ).astype(BF16)
    grad_up = (grad_active * gate_val * sigmoid_gate).astype(BF16)
    grad_both = jnp.concatenate([grad_gate, grad_up], axis=1)
    down_sum = scatter_chips(grad_down)
    grad_gate_up = matmul_rows(rows_two, grad_both).astype(BF16)
    normed_two_rows = return_rows(
        matmul_back(after(grad_both, grad_down), weight_gate_up), partners
    )
    gate_up_sum = scatter_chips(after(grad_gate_up, down_sum, *normed_two_rows))
    grad_gates_mlp = jnp.stack(
        [jnp.sum(grad_out * mlp_branch[choice], axis=-1) for choice in range(TOP)], axis=1
    )
    grad_logits_mlp = gate_back(gates_mlp, grad_gates_mlp, mlp_routes)
    grad_normed_two = matmul(
        jnp.sum(mlp_back, axis=0), jnp.concatenate(normed_two_rows)
    ) + exact_back(grad_logits_mlp, router_f[:, EXPERTS:])
    grad_hidden_norm, grad_gain_two = norm_back(hidden, inverse_two, gains_f[1], grad_normed_two)
    grad_hidden = grad_out + grad_hidden_norm
    grad_router_two = exact_rows(normed_two.astype(F32), grad_logits_mlp)

    rows_grad_attn = send_grads(attn_pick, gates_attn, attn_hit, grad_hidden, places)
    grad_project = matmul_rows(rows_grad_attn, attended).astype(BF16)
    grad_attended = matmul(rows_grad_attn, weight_project).astype(BF16)
    grad_gates_attn = jnp.stack(
        [jnp.sum(grad_hidden * branch[choice], axis=-1) for choice in range(TOP)], axis=1
    )
    grad_logits_attn = gate_back(gates_attn, grad_gates_attn, attn_routes)
    grad_heads = by_heads(per_sequence(pick_all, grad_attended, 1), sequences)
    grad_probs = heads_dot(grad_heads, value_heads, 3, 3)
    inner = jnp.sum(probs * grad_probs, axis=-1, keepdims=True)
    grad_scores = (probs * (grad_probs - inner)).astype(BF16)
    grad_query_heads = heads_dot(grad_scores, key_heads, 3, 2) * SCALE
    grad_key_heads = heads_dot(grad_scores, query_heads, 2, 2) * SCALE
    grad_value_heads = heads_dot(probs_low, grad_heads, 2, 2)
    back_tables = (tables[0], -tables[1])
    grad_query_pre = from_heads(rotate(grad_query_heads, *back_tables).astype(BF16))
    grad_keys = rotate(grad_key_heads, *back_tables).astype(BF16)
    grad_values = grad_value_heads.astype(BF16)
    grad_query = matmul_rows(normed_all, grad_query_pre).astype(BF16)
    def heads_of(step):
        start = (expert ^ step) * count
        return jnp.concatenate(
            [
                lax.dynamic_slice_in_dim(table, start, count, 0)
                for table in (grad_keys, grad_values)
            ]
        )

    grad_kv_parts = [heads_of(step) for step in range(EXPERTS)]
    grad_kv_parts[-1] = after(grad_kv_parts[-1], grad_query)
    grad_kv = sum(
        over_expert(part, step * halves).astype(F32) for step, part in enumerate(grad_kv_parts)
    ).astype(BF16)
    grad_kv = from_heads(grad_kv)
    grad_kv_weight = matmul_rows(normed_all, grad_kv).astype(BF16)
    normed_one_partial = matmul_back(grad_query_pre, weight_query) + matmul_back(
        grad_kv, kv_weight
    )
    grad_normed_router = exact_back(grad_logits_attn, router_f[:, :EXPERTS])
    grad_gain_one = jnp.sum(normed_one_partial * inputs_all * inverse_all, axis=0) + jnp.sum(
        grad_normed_router * inputs_f * inverse_one, axis=0
    )
    grad_small = jnp.concatenate(
        [
            exact_rows(normed_one.astype(F32), grad_logits_attn),
            grad_router_two,
            grad_gain_one[:, None],
            grad_gain_two[:, None],
        ],
        axis=1,
    ).astype(BF16)
    grad_small = jnp.pad(grad_small, ((0, 0), (0, LANES - grad_small.shape[1])))
    last_rows = fill(
        (grad_query.shape[0], 2 * width_attn + 2 * sixth + LANES),
        [
            (grad_project, 0, width_attn),
            (grad_query, 0, 0),
            (grad_kv_weight, 0, 2 * width_attn),
            (grad_small, 0, 2 * width_attn + 2 * sixth),
        ],
    )
    last_sum = scatter_chips(after(last_rows, gate_up_sum))
    gate_up_mine, gate_up_other = exchange_rows(core, gate_up_sum)
    reduced_gate_up = jnp.stack(
        [
            in_core_order(
                core,
                gate_up_mine[:, at * width_ff : (at + 1) * width_ff],
                gate_up_other[:, at * width_ff : (at + 1) * width_ff],
                1,
            )
            for at in range(2)
        ]
    )
    reduced_gate_up = with_layout_constraint(
        reduced_gate_up, Layout(major_to_minor=(0, 1, 2))
    ).astype(F32)
    update_gate_up = adam_step(moment_gate_up, square_gate_up, reduced_gate_up)
    normed_one_rows = return_rows(
        after(normed_one_partial, last_rows), partners, places, update_gate_up
    )
    grad_normed_one = sum(rows.astype(F32) for rows in normed_one_rows) + grad_normed_router
    grad_inputs_norm, _ = norm_back(inputs_f, inverse_one, gains_f[0], grad_normed_one)
    input_grad = grad_hidden + grad_inputs_norm

    down_sum, local_error, _ = together(down_sum, local_error, normed_one_rows)
    down_mine, down_other = exchange_rows(core, down_sum)
    reduced_down = turned(in_core_order(core, down_mine, down_other, 1))
    update_down = adam_step(moment_down, square_down, reduced_down)
    total_error = all_sum(local_error.reshape(1, 1))[0, 0]

    last_mine, last_other = exchange_rows(core, after(last_sum, total_error, *update_down))
    attn_mine, attn_other = last_mine[:, : 2 * width_attn], last_other[:, : 2 * width_attn]
    shared_mine, shared_theirs = [
        rows[:, 2 * width_attn :].reshape(partners, local_rows, -1)
        for rows in (last_mine, last_other)
    ]
    shared_pair = jnp.where(
        core == 0, jnp.stack([shared_mine, shared_theirs]), jnp.stack([shared_theirs, shared_mine])
    )
    received = jnp.stack(
        [
            over_expert(lax.dynamic_index_in_dim(shared_pair, expert_at ^ bits, 1, keepdims=False), bits)
            for bits in range(partners)
        ]
    )
    query_mine, project_mine = attn_mine[:, :width_attn], attn_mine[:, width_attn:]
    query_other, project_other = attn_other[:, :width_attn], attn_other[:, width_attn:]
    small_sum = jnp.sum(received[..., -LANES:].astype(F32), axis=(0, 1))
    received = jnp.stack(
        [lax.dynamic_index_in_dim(received, expert_at ^ at, 0, keepdims=False) for at in range(partners)]
    )
    reduced_kv = (
        received[..., :-LANES]
        .reshape(EXPERTS, halves, 2, local_rows, 2, sixth)
        .transpose(3, 4, 1, 2, 0, 5)
        .reshape(local_rows, -1)
        .astype(F32)
    )
    reduced_router = small_sum[:, : 2 * EXPERTS]
    reduced_gains = small_sum[:, 2 * EXPERTS : 2 * EXPERTS + 2].T
    reduced_query = with_layout_constraint(
        in_core_order(core, query_mine, query_other, 1), Layout(major_to_minor=(0, 1))
    ).astype(F32)
    reduced_project = turned(in_core_order(core, project_mine, project_other, 1))
    loss_value = total_error / total_count
    return (
        outputs,
        loss_value,
        input_grad,
        *adam_step(moment_query, square_query, reduced_query),
        *adam_step(moment_project, square_project, reduced_project),
        *update_gate_up,
        *update_down,
        *adam_step(moment_key_value, square_key_value, reduced_kv),
        *adam_step(moment_router, square_router, reduced_router),
        *adam_step(moment_gains, square_gains, reduced_gains),
    )


def solution(mesh):
    rows = P(("dp", "expert"), None)
    flat = P(("dp", "expert"))
    columns = P(None, ("dp", "expert"))
    query, project, gate_up = P("dp", "expert"), P("expert", "dp"), P(None, "dp", "expert")
    weights = (query, project, gate_up, project, rows, rows, columns)
    return jax.shard_map(
        body,
        mesh=mesh,
        in_specs=(rows, rows, rows, rows, flat, flat)
        + tuple(spec for spec in weights for _ in range(3)),
        out_specs=(rows, P(), rows) + tuple(spec for spec in weights for _ in range(4)),
        check_vma=False,
    )
```

```python
import jax
import jax.numpy as jnp
from jax import lax
from jax.experimental.layout import Layout, with_layout_constraint
from jax.sharding import PartitionSpec as P

D = 2048
HD = 128
EXPERTS = 4
TOP = 2
STEP = 10
QW = 2048
CAP = 96
LANES = 128

NORM_EPS = 1e-05
ADAM_EPS = 1e-08
BETA_FIRST = 0.9
BETA_SECOND = 0.95
ROPE_BASE = 10000.0
MASK_FILL = -1000000000.0
SCALE = HD ** (-0.5)
HIGHEST = lax.Precision.HIGHEST
F32 = jnp.float32
BF16 = jnp.bfloat16


def matmul(left_side, right_side):
    return jnp.dot(left_side, right_side, preferred_element_type=F32)


def matmul_back(left_side, right_side):
    return lax.dot_general(
        left_side, right_side, (((1,), (1,)), ((), ())), preferred_element_type=F32
    )


def matmul_rows(left_side, right_side):
    return lax.dot_general(
        left_side, right_side, (((0,), (0,)), ((), ())), preferred_element_type=F32
    )


def exact_back(left_side, right_side):
    return lax.dot_general(
        left_side,
        right_side,
        (((1,), (1,)), ((), ())),
        precision=HIGHEST,
        preferred_element_type=F32,
    )


def exact_rows(left_side, right_side):
    return lax.dot_general(
        left_side,
        right_side,
        (((0,), (0,)), ((), ())),
        precision=HIGHEST,
        preferred_element_type=F32,
    )


def rope_tables(length):
    half_dim = HD // 2
    frequency = ROPE_BASE ** (-(2.0 * jnp.arange(half_dim, dtype=F32)) / HD)
    angles = jnp.arange(length, dtype=F32)[:, None] * frequency[None, :]
    cosine, sine = jnp.cos(angles), jnp.sin(angles)
    return (
        jnp.concatenate([cosine, cosine], axis=1),
        jnp.concatenate([-sine, sine], axis=1),
    )


def swap_perm(count, bits):
    return [(place, place ^ bits) for place in range(count)]


def core_swap(value):
    return lax.ppermute(value, "dp", swap_perm(lax.axis_size("dp"), 1))


def over_expert(value, bits):
    if bits == 0:
        return value
    return lax.ppermute(value, "expert", swap_perm(lax.axis_size("expert"), bits))


def chip_groups():
    count = lax.axis_size("dp")
    return [[2 * place + core for place in range(count // 2)] for core in range(2)]


def gather_chips(block):
    return lax.all_gather(block, "dp", axis=0, tiled=True, axis_index_groups=chip_groups())


def scatter_chips(partial):
    return lax.psum_scatter(
        partial, "dp", scatter_dimension=0, tiled=True, axis_index_groups=chip_groups()
    )


def in_core_order(core, mine, other, axis):
    return jnp.where(
        core == 0,
        jnp.concatenate([mine, other], axis=axis),
        jnp.concatenate([other, mine], axis=axis),
    )


def halves_of(core, whole):
    width = whole.shape[-1] // 2
    return tuple(
        lax.dynamic_slice_in_dim(whole, at * width, width, whole.ndim - 1) for at in (core, 1 - core)
    )


def fill(shape, parts):
    buffer = jnp.zeros(shape, BF16)
    for part, row, column in parts:
        buffer = lax.dynamic_update_slice(buffer, part, (row, column))
    return buffer


def exchange_rows(core, summed):
    rows = summed.shape[0] // 2
    mine, theirs = [
        lax.dynamic_slice_in_dim(summed, at * rows, rows, 0) for at in (core, 1 - core)
    ]
    return (mine, core_swap(theirs))


def slots_before(hits):
    count = hits.shape[-2]
    place = jnp.arange(count, dtype=jnp.int32)
    earlier = (place[:, None] > place[None, :]).astype(BF16)
    return jnp.einsum(
        "ts,...sn->...tn", earlier, hits.astype(BF16), preferred_element_type=F32
    ).astype(jnp.int32)


def route_tables(routes, names):
    hit = routes[:, :, None] == names[None, None, :]
    named = jnp.any(hit, axis=1)
    slot = slots_before(named)
    at_slot = slot[:, :, None] == jnp.arange(CAP, dtype=jnp.int32)[None, None, :]
    pick = (named[:, :, None] & at_slot).astype(BF16).transpose(1, 2, 0)
    back = (hit[:, :, :, None] & at_slot[:, None]).astype(BF16)
    back = back.transpose(1, 0, 2, 3).reshape(TOP, routes.shape[0], -1)
    return (pick, back, hit.astype(F32))


def chosen_gates(logits, routes):
    hit = routes[:, :, None] == jnp.arange(EXPERTS, dtype=jnp.int32)[None, None, :]
    picked = jnp.sum(jnp.where(hit, logits[:, None, :], 0.0), axis=2)
    return jax.nn.softmax(picked, axis=-1)


def gate_back(gates, grad_gates, routes):
    hit = routes[:, :, None] == jnp.arange(EXPERTS, dtype=jnp.int32)[None, None, :]
    centred = gates * (grad_gates - jnp.sum(gates * grad_gates, axis=-1, keepdims=True))
    return jnp.sum(centred[:, :, None] * hit.astype(F32), axis=1)


def norm_back(values, inverse, gain_row, grad_normed):
    scaled = gain_row * grad_normed
    grad_values = inverse * scaled - values * inverse**3 * jnp.mean(
        scaled * values, axis=-1, keepdims=True
    )
    grad_gain = jnp.sum(grad_normed * values * inverse, axis=0)
    return (grad_values, grad_gain)


def place_rows(blocks, places):
    rows, width = blocks[0].shape
    got = jnp.zeros((len(blocks) * rows, width), blocks[0].dtype)
    for block, place in zip(blocks, places):
        got = lax.dynamic_update_slice_in_dim(got, block, place * rows, 0)
    return jnp.concatenate([got, core_swap(got)])


def send_rows(blocks, places=None):
    blocks = [over_expert(block, bits) for bits, block in enumerate(blocks)]
    return place_rows(blocks, range(len(blocks)) if places is None else places)


def return_rows(partial, partners, places=None, between=()):
    count = partial.shape[0] // 2
    got = core_swap(partial[count:].astype(BF16))
    summed = (partial[:count].astype(F32) + got.astype(F32)).astype(BF16)
    rows = count // partners
    places = range(partners) if places is None else places
    blocks = [lax.dynamic_slice_in_dim(summed, place * rows, rows, 0) for place in places]
    blocks[-1] = after(blocks[-1], *between)
    return [over_expert(block, bits) for bits, block in enumerate(blocks)]


def over_chips(value, bits):
    if bits == 0:
        return value
    return lax.ppermute(value, "dp", swap_perm(lax.axis_size("dp"), 2 * bits))


def gather_small(chip, block):
    count, rows = lax.axis_size("dp") // 2, block.shape[0]
    whole = jnp.zeros((count * rows, block.shape[1]), block.dtype)
    for bits in range(count):
        whole = lax.dynamic_update_slice_in_dim(
            whole, over_chips(block, bits), (chip ^ bits) * rows, 0
        )
    return whole


def gather_split(chip, block):
    if lax.axis_size("dp") != 8:
        return gather_small(chip, block)
    rows = block.shape[0]
    middle = rows // 2
    across, along = over_chips(block, 1), over_chips(block, 2)
    pieces = [
        (block, chip, 0),
        (across, chip ^ 1, 0),
        (along, chip ^ 2, 0),
        (over_chips(across[:middle], 2), chip ^ 3, 0),
        (over_chips(along[middle:], 1), chip ^ 3, middle),
    ]
    whole = jnp.zeros((4 * rows, block.shape[1]), block.dtype)
    for piece, place, start in pieces:
        whole = lax.dynamic_update_slice_in_dim(whole, piece, place * rows + start, 0)
    return whole


def rotate(value, cosine, sine):
    half_dim = HD // 2
    swapped = jnp.concatenate([value[..., half_dim:], value[..., :half_dim]], axis=-1)
    return value * cosine + swapped * sine


def by_heads(rows, sequences):
    heads = rows.shape[1] // HD
    return rows.reshape(-1, heads, HD).transpose(1, 0, 2).reshape(heads, sequences, -1, HD)


def from_heads(blocks):
    heads = blocks.shape[0]
    return blocks.reshape(heads, -1, HD).transpose(1, 0, 2).reshape(-1, heads * HD)


def heads_dot(left_side, right_side, left_axis, right_axis):
    return lax.dot_general(
        left_side,
        right_side,
        (((left_axis,), (right_axis,)), ((0, 1), (0, 1))),
        preferred_element_type=F32,
    )


def turned(rows):
    return with_layout_constraint(rows.T.astype(F32), Layout(major_to_minor=(0, 1)))


def all_sum(value):
    bits = 1
    while bits < lax.axis_size("dp"):
        value = value + lax.ppermute(value, "dp", swap_perm(lax.axis_size("dp"), bits))
        bits *= 2
    bits = 1
    while bits < lax.axis_size("expert"):
        value = value + over_expert(value, bits)
        bits *= 2
    return value


def after(value, *others):
    return lax.optimization_barrier((value, *others))[0]


def together(*groups):
    return lax.optimization_barrier(groups)


def adam_step(moment, square, gradient):
    moment_new = BETA_FIRST * moment + (1.0 - BETA_FIRST) * gradient
    square_new = BETA_SECOND * square + (1.0 - BETA_SECOND) * gradient * gradient
    moment_hat = moment_new / (1.0 - BETA_FIRST**STEP)
    square_hat = square_new / (1.0 - BETA_SECOND**STEP)
    direction = moment_hat / (jnp.sqrt(square_hat) + ADAM_EPS)
    return (gradient, direction, moment_new, square_new)


def body(
    tokens,
    teacher,
    attn_routes,
    mlp_routes,
    image_mask,
    valid,
    master_query,
    moment_query,
    square_query,
    master_project,
    moment_project,
    square_project,
    master_gate_up,
    moment_gate_up,
    square_gate_up,
    master_down,
    moment_down,
    square_down,
    master_key_value,
    moment_key_value,
    square_key_value,
    master_router,
    moment_router,
    square_router,
    master_gains,
    moment_gains,
    square_gains,
):
    partners = lax.axis_size("expert")
    halves = partners // EXPERTS
    core, chip = lax.axis_index("dp") % 2, lax.axis_index("dp") // 2
    expert_at = lax.axis_index("expert")
    expert, half = expert_at // halves, expert_at % halves
    names = (expert_at ^ jnp.arange(partners, dtype=jnp.int32)) // halves
    token_count = tokens.shape[0]
    sequences = 2 * partners
    sixth = master_query.shape[1] // (2 * EXPERTS)

    valid_f = valid.astype(F32)
    marks = jnp.concatenate([attn_routes, image_mask[:, None]], axis=1).astype(BF16)
    marks = jnp.pad(marks, ((0, 0), (0, LANES - marks.shape[1])))
    payload = jnp.concatenate([tokens, marks], axis=1)
    places = [expert_at ^ bits for bits in range(partners)]

    map_rows = master_query.shape[0]
    row_mine, row_got = core * map_rows, (1 - core) * map_rows
    query_mine, query_theirs = halves_of(core, master_query)
    project_mine, project_theirs = halves_of(core, master_project.astype(BF16).T)
    width_attn = query_mine.shape[1]
    attn_rows = fill(
        (2 * map_rows, 2 * width_attn),
        [
            (query_mine.astype(BF16), row_mine, 0),
            (project_mine, row_mine, width_attn),
            (core_swap(query_theirs.astype(BF16)), row_got, 0),
            (core_swap(project_theirs), row_got, width_attn),
        ],
    )
    weight_attn = gather_chips(attn_rows)
    weight_query, weight_project = weight_attn[:, :width_attn], weight_attn[:, width_attn:]

    local_rows = master_key_value.shape[0]
    small = jnp.concatenate(
        [
            master_router,
            master_gains.T,
            jnp.full((local_rows, 1), jnp.sum(valid_f)),
        ],
        axis=1,
    ).astype(BF16)
    small = jnp.pad(small, ((0, 0), (0, LANES - small.shape[1])))
    half_width = EXPERTS * sixth

    def for_core(at):
        return jnp.concatenate(
            [
                lax.dynamic_slice_in_dim(
                    master_key_value, side * QW + (2 * part + at) * half_width, half_width, 1
                )
                for side in range(2)
                for part in range(halves)
            ],
            axis=1,
        ).astype(BF16)

    kv_mine = jnp.concatenate([for_core(core), small], axis=1)
    kv_got = core_swap(jnp.concatenate([for_core(1 - core), small], axis=1))

    def block_for(rows, bits):
        other = expert_at ^ bits
        column = ((other % halves) * EXPERTS + other // halves) * sixth
        return jnp.concatenate(
            [
                lax.dynamic_slice_in_dim(rows, column, sixth, 1),
                lax.dynamic_slice_in_dim(rows, halves * half_width + column, sixth, 1),
                rows[:, 2 * halves * half_width :],
            ],
            axis=1,
        )

    kv_pair = in_core_order(core, kv_mine, kv_got, 0)
    kv_blocks = [block_for(kv_pair, bits) for bits in range(partners)]

    width_ff = master_gate_up.shape[2] // 2
    kv_blocks = [over_expert(block, bits) for bits, block in enumerate(kv_blocks)]
    kv_blocks, payload = together(kv_blocks, payload)
    token_blocks = [over_expert(payload, bits) for bits in range(partners)]
    arrived = jnp.zeros((2 * partners * local_rows, 2 * sixth + LANES), BF16)
    for block, at in zip(kv_blocks, places):
        arrived = lax.dynamic_update_slice_in_dim(arrived, block, at * 2 * local_rows, 0)
    arrived = arrived.reshape(partners, 2, local_rows, -1).transpose(1, 0, 2, 3)
    arrived = arrived.reshape(2 * partners * local_rows, -1)
    arrived, master_gate_up, _ = together(arrived, master_gate_up, attn_rows)
    gate_mine, gate_theirs = halves_of(core, master_gate_up[0])
    up_mine, up_theirs = halves_of(core, master_gate_up[1])
    gate_up_rows = fill(
        (2 * map_rows, 2 * width_ff),
        [
            (gate_mine.astype(BF16), row_mine, 0),
            (up_mine.astype(BF16), row_mine, width_ff),
            (core_swap(gate_theirs.astype(BF16)), row_got, 0),
            (core_swap(up_theirs.astype(BF16)), row_got, width_ff),
        ],
    )
    shared_whole = gather_split(chip, arrived)
    shared_whole, token_blocks, _ = together(shared_whole, token_blocks, gate_up_rows)
    everyone = place_rows(token_blocks, places)
    kv_weight = shared_whole[:, : 2 * sixth]
    small_whole = shared_whole[:, 2 * sixth :]
    router_low = small_whole[:, : 2 * EXPERTS]
    router_f = router_low.astype(F32)
    gains_f = small_whole[:, 2 * EXPERTS : 2 * EXPERTS + 2].astype(F32).T
    total_count = jnp.sum(small_whole[:, 2 * EXPERTS + 2].astype(F32)) / local_rows

    weight_gate_up = gather_chips(gate_up_rows)
    down_mine, down_theirs = halves_of(core, master_down.astype(BF16).T)
    down_rows = fill(
        (2 * map_rows, width_ff),
        [(down_mine, row_mine, 0), (core_swap(down_theirs), row_got, 0)],
    )
    weight_down = gather_chips(down_rows)

    tables = rope_tables(token_count)
    inputs_all = everyone[:, :D].astype(F32)
    inverse_all = lax.rsqrt(jnp.mean(inputs_all * inputs_all, axis=-1, keepdims=True) + NORM_EPS)
    normed_all = (inputs_all * inverse_all * gains_f[0]).astype(BF16)
    inputs_f = tokens.astype(F32)
    inverse_one, normed_one = (
        lax.dynamic_slice_in_dim(table, expert_at * token_count, token_count, 0)
        for table in (inverse_all, normed_all)
    )
    marks_all = everyone[:, D:].astype(F32).reshape(sequences, token_count, LANES)
    named_all = jnp.any(marks_all[:, :, :TOP] == expert.astype(F32), axis=2)
    slot_all = slots_before(named_all[:, :, None])[:, :, 0]
    slots = jnp.arange(CAP, dtype=jnp.int32)
    pick_all = (named_all[:, None, :] & (slot_all[:, None, :] == slots[None, :, None])).astype(BF16)
    image_on = marks_all[:, :, TOP] > 0.0
    position = jnp.arange(token_count, dtype=jnp.int32)
    allowed = (position[:, None] >= position[None, :])[None] | (
        image_on[:, :, None] & image_on[:, None, :]
    )

    kv_heads = by_heads(matmul(normed_all, kv_weight), sequences)
    count = sixth // HD
    kv_own = jnp.concatenate(
        [rotate(kv_heads[:count], *tables).astype(BF16), kv_heads[count:].astype(BF16)]
    )
    query_pre = matmul(normed_all, weight_query)
    query_heads = rotate(by_heads(query_pre, sequences), *tables).astype(BF16)
    kv_shared = [over_expert(kv_own, step * halves) for step in range(EXPERTS - 1)]
    kv_shared.append(over_expert(after(kv_own, query_heads, down_rows), (EXPERTS - 1) * halves))

    def every_head(parts):
        whole = jnp.zeros((EXPERTS * count,) + parts[0].shape[1:], BF16)
        for step, part in enumerate(parts):
            whole = lax.dynamic_update_slice_in_dim(whole, part, (expert ^ step) * count, 0)
        return whole

    key_heads = every_head([part[:count] for part in kv_shared])
    value_heads = every_head([part[count:] for part in kv_shared])
    scores = heads_dot(query_heads, key_heads, 3, 3) * SCALE
    scores = jnp.where(allowed[None], scores, MASK_FILL)
    probs = jax.nn.softmax(scores, axis=-1)
    probs_low = probs.astype(BF16)
    attended_all = from_heads(heads_dot(probs_low, value_heads, 3, 2).astype(BF16))

    def per_sequence(table, rows, left_axis):
        blocks = rows.reshape(sequences, -1, rows.shape[1])
        picked = lax.dot_general(
            table, blocks, (((left_axis,), (1,)), ((0,), (0,))), preferred_element_type=F32
        )
        return picked.astype(BF16).reshape(-1, rows.shape[1])

    attended = per_sequence(pick_all, attended_all, 2)

    attn_pick, attn_back, attn_hit = route_tables(attn_routes, names)
    gates_attn = chosen_gates(matmul(normed_one, router_low[:, :EXPERTS]), attn_routes)
    branch_rows = jnp.concatenate(
        return_rows(matmul_back(attended, weight_project), partners, places)
    )
    branch = [matmul(attn_back[choice], branch_rows) for choice in range(TOP)]
    hidden = inputs_f + sum(gates_attn[:, choice, None] * branch[choice] for choice in range(TOP))

    inverse_two = lax.rsqrt(jnp.mean(hidden * hidden, axis=-1, keepdims=True) + NORM_EPS)
    normed_two = (hidden * inverse_two * gains_f[1]).astype(BF16)
    mlp_pick, mlp_back, mlp_hit = route_tables(mlp_routes, names)
    gates_mlp = chosen_gates(matmul(normed_two, router_low[:, EXPERTS:]), mlp_routes)
    placed = matmul(mlp_pick.reshape(-1, token_count), normed_two).astype(BF16)
    rows_two = send_rows(list(placed.reshape(partners, CAP, D)))
    gate_up_val = matmul(rows_two, weight_gate_up)
    gate_val, up_val = gate_up_val[:, :width_ff], gate_up_val[:, width_ff:]
    active = (jax.nn.silu(gate_val) * up_val).astype(BF16)
    mlp_rows = jnp.concatenate(return_rows(matmul_back(active, weight_down).astype(BF16), partners))
    mlp_branch = [matmul(mlp_back[choice], mlp_rows) for choice in range(TOP)]
    outputs = hidden + sum(gates_mlp[:, choice, None] * mlp_branch[choice] for choice in range(TOP))

    deviation = outputs - teacher.astype(F32)
    local_error = jnp.sum(valid_f[:, None] * deviation * deviation)
    grad_out = 2.0 * valid_f[:, None] * deviation / total_count

    def send_grads(pick, gates, hit, grad, where=None):
        gate_of = jnp.sum(gates[:, :, None] * hit, axis=1)
        rows = (gate_of.T[:, :, None] * grad[None]).astype(BF16)
        sent = jnp.einsum("kct,ktd->kcd", pick, rows, preferred_element_type=F32).astype(BF16)
        return send_rows(list(sent), where)

    rows_grad = send_grads(mlp_pick, gates_mlp, mlp_hit, grad_out)
    grad_down = matmul_rows(rows_grad, active).astype(BF16)
    grad_active = matmul(rows_grad, weight_down)
    sigmoid_gate = jax.nn.sigmoid(gate_val)
    grad_gate = (
        grad_active * up_val * sigmoid_gate * (1.0 + gate_val * (1.0 - sigmoid_gate))
    ).astype(BF16)
    grad_up = (grad_active * gate_val * sigmoid_gate).astype(BF16)
    grad_both = jnp.concatenate([grad_gate, grad_up], axis=1)
    down_sum = scatter_chips(grad_down)
    grad_gate_up = matmul_rows(rows_two, grad_both).astype(BF16)
    normed_two_rows = return_rows(
        matmul_back(after(grad_both, grad_down), weight_gate_up), partners
    )
    gate_up_sum = scatter_chips(after(grad_gate_up, down_sum, *normed_two_rows))
    grad_gates_mlp = jnp.stack(
        [jnp.sum(grad_out * mlp_branch[choice], axis=-1) for choice in range(TOP)], axis=1
    )
    grad_logits_mlp = gate_back(gates_mlp, grad_gates_mlp, mlp_routes)
    grad_normed_two = matmul(
        jnp.sum(mlp_back, axis=0), jnp.concatenate(normed_two_rows)
    ) + exact_back(grad_logits_mlp, router_f[:, EXPERTS:])
    grad_hidden_norm, grad_gain_two = norm_back(hidden, inverse_two, gains_f[1], grad_normed_two)
    grad_hidden = grad_out + grad_hidden_norm
    grad_router_two = exact_rows(normed_two.astype(F32), grad_logits_mlp)

    rows_grad_attn = send_grads(attn_pick, gates_attn, attn_hit, grad_hidden, places)
    grad_project = matmul_rows(rows_grad_attn, attended).astype(BF16)
    grad_attended = matmul(rows_grad_attn, weight_project).astype(BF16)
    grad_gates_attn = jnp.stack(
        [jnp.sum(grad_hidden * branch[choice], axis=-1) for choice in range(TOP)], axis=1
    )
    grad_logits_attn = gate_back(gates_attn, grad_gates_attn, attn_routes)
    grad_heads = by_heads(per_sequence(pick_all, grad_attended, 1), sequences)
    grad_probs = heads_dot(grad_heads, value_heads, 3, 3)
    inner = jnp.sum(probs * grad_probs, axis=-1, keepdims=True)
    grad_scores = (probs * (grad_probs - inner)).astype(BF16)
    grad_query_heads = heads_dot(grad_scores, key_heads, 3, 2) * SCALE
    grad_key_heads = heads_dot(grad_scores, query_heads, 2, 2) * SCALE
    grad_value_heads = heads_dot(probs_low, grad_heads, 2, 2)
    back_tables = (tables[0], -tables[1])
    grad_query_pre = from_heads(rotate(grad_query_heads, *back_tables).astype(BF16))
    grad_keys = rotate(grad_key_heads, *back_tables).astype(BF16)
    grad_values = grad_value_heads.astype(BF16)
    grad_query = matmul_rows(normed_all, grad_query_pre).astype(BF16)
    def heads_of(step):
        start = (expert ^ step) * count
        return jnp.concatenate(
            [
                lax.dynamic_slice_in_dim(table, start, count, 0)
                for table in (grad_keys, grad_values)
            ]
        )

    grad_kv_parts = [heads_of(step) for step in range(EXPERTS)]
    grad_kv_parts[-1] = after(grad_kv_parts[-1], grad_query)
    grad_kv = sum(
        over_expert(part, step * halves).astype(F32) for step, part in enumerate(grad_kv_parts)
    ).astype(BF16)
    grad_kv = from_heads(grad_kv)
    grad_kv_weight = matmul_rows(normed_all, grad_kv).astype(BF16)
    normed_one_partial = matmul_back(grad_query_pre, weight_query) + matmul_back(
        grad_kv, kv_weight
    )
    grad_normed_router = exact_back(grad_logits_attn, router_f[:, :EXPERTS])
    grad_gain_one = jnp.sum(normed_one_partial * inputs_all * inverse_all, axis=0) + jnp.sum(
        grad_normed_router * inputs_f * inverse_one, axis=0
    )
    grad_small = jnp.concatenate(
        [
            exact_rows(normed_one.astype(F32), grad_logits_attn),
            grad_router_two,
            grad_gain_one[:, None],
            grad_gain_two[:, None],
        ],
        axis=1,
    ).astype(BF16)
    grad_small = jnp.pad(grad_small, ((0, 0), (0, LANES - grad_small.shape[1])))
    last_rows = fill(
        (grad_query.shape[0], 2 * width_attn + 2 * sixth + LANES),
        [
            (grad_project, 0, width_attn),
            (grad_query, 0, 0),
            (grad_kv_weight, 0, 2 * width_attn),
            (grad_small, 0, 2 * width_attn + 2 * sixth),
        ],
    )
    last_sum = scatter_chips(after(last_rows, gate_up_sum))
    gate_up_mine, gate_up_other = exchange_rows(core, gate_up_sum)
    reduced_gate_up = jnp.stack(
        [
            in_core_order(
                core,
                gate_up_mine[:, at * width_ff : (at + 1) * width_ff],
                gate_up_other[:, at * width_ff : (at + 1) * width_ff],
                1,
            )
            for at in range(2)
        ]
    )
    reduced_gate_up = with_layout_constraint(
        reduced_gate_up, Layout(major_to_minor=(0, 1, 2))
    ).astype(F32)
    update_gate_up = adam_step(moment_gate_up, square_gate_up, reduced_gate_up)
    normed_one_rows = return_rows(
        after(normed_one_partial, last_rows), partners, places, update_gate_up
    )
    grad_normed_one = sum(rows.astype(F32) for rows in normed_one_rows) + grad_normed_router
    grad_inputs_norm, _ = norm_back(inputs_f, inverse_one, gains_f[0], grad_normed_one)
    input_grad = grad_hidden + grad_inputs_norm

    down_sum, local_error, _ = together(down_sum, local_error, normed_one_rows)
    down_mine, down_other = exchange_rows(core, down_sum)
    reduced_down = turned(in_core_order(core, down_mine, down_other, 1))
    update_down = adam_step(moment_down, square_down, reduced_down)
    total_error = all_sum(local_error.reshape(1, 1))[0, 0]

    last_mine, last_other = exchange_rows(core, after(last_sum, total_error, *update_down))
    attn_mine, attn_other = last_mine[:, : 2 * width_attn], last_other[:, : 2 * width_attn]
    shared_mine, shared_theirs = [
        rows[:, 2 * width_attn :].reshape(partners, local_rows, -1)
        for rows in (last_mine, last_other)
    ]
    shared_pair = jnp.where(
        core == 0, jnp.stack([shared_mine, shared_theirs]), jnp.stack([shared_theirs, shared_mine])
    )
    received = jnp.stack(
        [
            over_expert(lax.dynamic_index_in_dim(shared_pair, expert_at ^ bits, 1, keepdims=False), bits)
            for bits in range(partners)
        ]
    )
    query_mine, project_mine = attn_mine[:, :width_attn], attn_mine[:, width_attn:]
    query_other, project_other = attn_other[:, :width_attn], attn_other[:, width_attn:]
    small_sum = jnp.sum(received[..., -LANES:].astype(F32), axis=(0, 1))
    received = jnp.stack(
        [lax.dynamic_index_in_dim(received, expert_at ^ at, 0, keepdims=False) for at in range(partners)]
    )
    reduced_kv = (
        received[..., :-LANES]
        .reshape(EXPERTS, halves, 2, local_rows, 2, sixth)
        .transpose(3, 4, 1, 2, 0, 5)
        .reshape(local_rows, -1)
        .astype(F32)
    )
    reduced_router = small_sum[:, : 2 * EXPERTS]
    reduced_gains = small_sum[:, 2 * EXPERTS : 2 * EXPERTS + 2].T
    reduced_query = with_layout_constraint(
        in_core_order(core, query_mine, query_other, 1), Layout(major_to_minor=(0, 1))
    ).astype(F32)
    reduced_project = turned(in_core_order(core, project_mine, project_other, 1))
    loss_value = total_error / total_count
    return (
        outputs,
        loss_value,
        input_grad,
        *adam_step(moment_query, square_query, reduced_query),
        *adam_step(moment_project, square_project, reduced_project),
        *update_gate_up,
        *update_down,
        *adam_step(moment_key_value, square_key_value, reduced_kv),
        *adam_step(moment_router, square_router, reduced_router),
        *adam_step(moment_gains, square_gains, reduced_gains),
    )


def solution(mesh):
    rows = P(("dp", "expert"), None)
    flat = P(("dp", "expert"))
    columns = P(None, ("dp", "expert"))
    query, project, gate_up = P("dp", "expert"), P("expert", "dp"), P(None, "dp", "expert")
    weights = (query, project, gate_up, project, rows, rows, columns)
    return jax.shard_map(
        body,
        mesh=mesh,
        in_specs=(rows, rows, rows, rows, flat, flat)
        + tuple(spec for spec in weights for _ in range(3)),
        out_specs=(rows, P(), rows) + tuple(spec for spec in weights for _ in range(4)),
        check_vma=False,
    )
```

```python
import jax
import jax.numpy as jnp
from jax import lax
from jax.experimental.layout import Layout, with_layout_constraint
from jax.sharding import PartitionSpec as P

D = 2048
HD = 128
EXPERTS = 4
TOP = 2
STEP = 10
QW = 2048
CAP = 96
LANES = 128

NORM_EPS = 1e-05
ADAM_EPS = 1e-08
BETA_FIRST = 0.9
BETA_SECOND = 0.95
ROPE_BASE = 10000.0
MASK_FILL = -1000000000.0
SCALE = HD ** (-0.5)
HIGHEST = lax.Precision.HIGHEST
F32 = jnp.float32
BF16 = jnp.bfloat16


def matmul(left_side, right_side):
    return jnp.dot(left_side, right_side, preferred_element_type=F32)


def matmul_back(left_side, right_side):
    return lax.dot_general(
        left_side, right_side, (((1,), (1,)), ((), ())), preferred_element_type=F32
    )


def matmul_rows(left_side, right_side):
    return lax.dot_general(
        left_side, right_side, (((0,), (0,)), ((), ())), preferred_element_type=F32
    )


def exact_back(left_side, right_side):
    return lax.dot_general(
        left_side,
        right_side,
        (((1,), (1,)), ((), ())),
        precision=HIGHEST,
        preferred_element_type=F32,
    )


def exact_rows(left_side, right_side):
    return lax.dot_general(
        left_side,
        right_side,
        (((0,), (0,)), ((), ())),
        precision=HIGHEST,
        preferred_element_type=F32,
    )


def rope_tables(length):
    half_dim = HD // 2
    frequency = ROPE_BASE ** (-(2.0 * jnp.arange(half_dim, dtype=F32)) / HD)
    angles = jnp.arange(length, dtype=F32)[:, None] * frequency[None, :]
    cosine, sine = jnp.cos(angles), jnp.sin(angles)
    return (
        jnp.concatenate([cosine, cosine], axis=1),
        jnp.concatenate([-sine, sine], axis=1),
    )


def swap_perm(count, bits):
    return [(place, place ^ bits) for place in range(count)]


def core_swap(value):
    return lax.ppermute(value, "dp", swap_perm(lax.axis_size("dp"), 1))


def over_expert(value, bits):
    if bits == 0:
        return value
    return lax.ppermute(value, "expert", swap_perm(lax.axis_size("expert"), bits))


def chip_groups():
    count = lax.axis_size("dp")
    return [[2 * place + core for place in range(count // 2)] for core in range(2)]


def gather_chips(block):
    return lax.all_gather(block, "dp", axis=0, tiled=True, axis_index_groups=chip_groups())


def scatter_chips(partial):
    return lax.psum_scatter(
        partial, "dp", scatter_dimension=0, tiled=True, axis_index_groups=chip_groups()
    )


def in_core_order(core, mine, other, axis):
    return jnp.where(
        core == 0,
        jnp.concatenate([mine, other], axis=axis),
        jnp.concatenate([other, mine], axis=axis),
    )


def halves_of(core, whole):
    width = whole.shape[-1] // 2
    return tuple(
        lax.dynamic_slice_in_dim(whole, at * width, width, whole.ndim - 1) for at in (core, 1 - core)
    )


def fill(shape, parts):
    buffer = jnp.zeros(shape, BF16)
    for part, row, column in parts:
        buffer = lax.dynamic_update_slice(buffer, part, (row, column))
    return buffer


def exchange_rows(core, summed):
    rows = summed.shape[0] // 2
    mine, theirs = [
        lax.dynamic_slice_in_dim(summed, at * rows, rows, 0) for at in (core, 1 - core)
    ]
    return (mine, core_swap(theirs))


def slots_before(hits):
    count = hits.shape[-2]
    place = jnp.arange(count, dtype=jnp.int32)
    earlier = (place[:, None] > place[None, :]).astype(BF16)
    return jnp.einsum(
        "ts,...sn->...tn", earlier, hits.astype(BF16), preferred_element_type=F32
    ).astype(jnp.int32)


def route_tables(routes, names):
    hit = routes[:, :, None] == names[None, None, :]
    named = jnp.any(hit, axis=1)
    slot = slots_before(named)
    at_slot = slot[:, :, None] == jnp.arange(CAP, dtype=jnp.int32)[None, None, :]
    pick = (named[:, :, None] & at_slot).astype(BF16).transpose(1, 2, 0)
    back = (hit[:, :, :, None] & at_slot[:, None]).astype(BF16)
    back = back.transpose(1, 0, 2, 3).reshape(TOP, routes.shape[0], -1)
    return (pick, back, hit.astype(F32))


def chosen_gates(logits, routes):
    hit = routes[:, :, None] == jnp.arange(EXPERTS, dtype=jnp.int32)[None, None, :]
    picked = jnp.sum(jnp.where(hit, logits[:, None, :], 0.0), axis=2)
    return jax.nn.softmax(picked, axis=-1)


def gate_back(gates, grad_gates, routes):
    hit = routes[:, :, None] == jnp.arange(EXPERTS, dtype=jnp.int32)[None, None, :]
    centred = gates * (grad_gates - jnp.sum(gates * grad_gates, axis=-1, keepdims=True))
    return jnp.sum(centred[:, :, None] * hit.astype(F32), axis=1)


def norm_back(values, inverse, gain_row, grad_normed):
    scaled = gain_row * grad_normed
    grad_values = inverse * scaled - values * inverse**3 * jnp.mean(
        scaled * values, axis=-1, keepdims=True
    )
    grad_gain = jnp.sum(grad_normed * values * inverse, axis=0)
    return (grad_values, grad_gain)


def place_rows(blocks, places):
    rows, width = blocks[0].shape
    got = jnp.zeros((len(blocks) * rows, width), blocks[0].dtype)
    for block, place in zip(blocks, places):
        got = lax.dynamic_update_slice_in_dim(got, block, place * rows, 0)
    return jnp.concatenate([got, core_swap(got)])


def send_rows(blocks, places=None, by_block=False):
    blocks = [over_expert(block, bits) for bits, block in enumerate(blocks)]
    if by_block:
        return jnp.concatenate(blocks + [core_swap(block) for block in blocks])
    return place_rows(blocks, range(len(blocks)) if places is None else places)


def return_rows(partial, partners, places=None, between=()):
    count = partial.shape[0] // 2
    got = core_swap(partial[count:].astype(BF16))
    summed = (partial[:count].astype(F32) + got.astype(F32)).astype(BF16)
    rows = count // partners
    places = range(partners) if places is None else places
    blocks = [lax.dynamic_slice_in_dim(summed, place * rows, rows, 0) for place in places]
    blocks[-1] = after(blocks[-1], *between)
    return [over_expert(block, bits) for bits, block in enumerate(blocks)]


def over_chips(value, bits):
    if bits == 0:
        return value
    return lax.ppermute(value, "dp", swap_perm(lax.axis_size("dp"), 2 * bits))


def gather_small(chip, block):
    count, rows = lax.axis_size("dp") // 2, block.shape[0]
    whole = jnp.zeros((count * rows, block.shape[1]), block.dtype)
    for bits in range(count):
        whole = lax.dynamic_update_slice_in_dim(
            whole, over_chips(block, bits), (chip ^ bits) * rows, 0
        )
    return whole


def gather_split(chip, block):
    if lax.axis_size("dp") != 8:
        return gather_small(chip, block)
    rows = block.shape[0]
    middle = rows // 2
    across, along = over_chips(block, 1), over_chips(block, 2)
    pieces = [
        (block, chip, 0),
        (across, chip ^ 1, 0),
        (along, chip ^ 2, 0),
        (over_chips(across[:middle], 2), chip ^ 3, 0),
        (over_chips(along[middle:], 1), chip ^ 3, middle),
    ]
    whole = jnp.zeros((4 * rows, block.shape[1]), block.dtype)
    for piece, place, start in pieces:
        whole = lax.dynamic_update_slice_in_dim(whole, piece, place * rows + start, 0)
    return whole


def rotate(value, cosine, sine):
    half_dim = HD // 2
    swapped = jnp.concatenate([value[..., half_dim:], value[..., :half_dim]], axis=-1)
    return value * cosine + swapped * sine


def by_heads(rows, sequences):
    heads = rows.shape[1] // HD
    return rows.reshape(-1, heads, HD).transpose(1, 0, 2).reshape(heads, sequences, -1, HD)


def from_heads(blocks):
    heads = blocks.shape[0]
    return blocks.reshape(heads, -1, HD).transpose(1, 0, 2).reshape(-1, heads * HD)


def heads_dot(left_side, right_side, left_axis, right_axis):
    return lax.dot_general(
        left_side,
        right_side,
        (((left_axis,), (right_axis,)), ((0, 1), (0, 1))),
        preferred_element_type=F32,
    )


def turned(rows):
    return with_layout_constraint(rows.T.astype(F32), Layout(major_to_minor=(0, 1)))


def all_sum(value):
    bits = 1
    while bits < lax.axis_size("dp"):
        value = value + lax.ppermute(value, "dp", swap_perm(lax.axis_size("dp"), bits))
        bits *= 2
    bits = 1
    while bits < lax.axis_size("expert"):
        value = value + over_expert(value, bits)
        bits *= 2
    return value


def after(value, *others):
    return lax.optimization_barrier((value, *others))[0]


def together(*groups):
    return lax.optimization_barrier(groups)


def adam_step(moment, square, gradient):
    moment_new = BETA_FIRST * moment + (1.0 - BETA_FIRST) * gradient
    square_new = BETA_SECOND * square + (1.0 - BETA_SECOND) * gradient * gradient
    moment_hat = moment_new / (1.0 - BETA_FIRST**STEP)
    square_hat = square_new / (1.0 - BETA_SECOND**STEP)
    direction = moment_hat / (jnp.sqrt(square_hat) + ADAM_EPS)
    return (gradient, direction, moment_new, square_new)


def body(
    tokens,
    teacher,
    attn_routes,
    mlp_routes,
    image_mask,
    valid,
    master_query,
    moment_query,
    square_query,
    master_project,
    moment_project,
    square_project,
    master_gate_up,
    moment_gate_up,
    square_gate_up,
    master_down,
    moment_down,
    square_down,
    master_key_value,
    moment_key_value,
    square_key_value,
    master_router,
    moment_router,
    square_router,
    master_gains,
    moment_gains,
    square_gains,
):
    partners = lax.axis_size("expert")
    halves = partners // EXPERTS
    core, chip = lax.axis_index("dp") % 2, lax.axis_index("dp") // 2
    expert_at = lax.axis_index("expert")
    expert, half = expert_at // halves, expert_at % halves
    names = (expert_at ^ jnp.arange(partners, dtype=jnp.int32)) // halves
    token_count = tokens.shape[0]
    sequences = 2 * partners
    sixth = master_query.shape[1] // (2 * EXPERTS)

    valid_f = valid.astype(F32)
    marks = jnp.concatenate([attn_routes, image_mask[:, None]], axis=1).astype(BF16)
    marks = jnp.pad(marks, ((0, 0), (0, LANES - marks.shape[1])))
    payload = jnp.concatenate([tokens, marks], axis=1)
    places = [expert_at ^ bits for bits in range(partners)]

    map_rows = master_query.shape[0]
    row_mine, row_got = core * map_rows, (1 - core) * map_rows
    query_mine, query_theirs = halves_of(core, master_query)
    project_mine, project_theirs = halves_of(core, master_project.astype(BF16).T)
    width_attn = query_mine.shape[1]
    attn_rows = fill(
        (2 * map_rows, 2 * width_attn),
        [
            (query_mine.astype(BF16), row_mine, 0),
            (project_mine, row_mine, width_attn),
            (core_swap(query_theirs.astype(BF16)), row_got, 0),
            (core_swap(project_theirs), row_got, width_attn),
        ],
    )
    weight_attn = gather_chips(attn_rows)
    weight_query, weight_project = weight_attn[:, :width_attn], weight_attn[:, width_attn:]

    local_rows = master_key_value.shape[0]
    small = jnp.concatenate(
        [
            master_router,
            master_gains.T,
            jnp.full((local_rows, 1), jnp.sum(valid_f)),
        ],
        axis=1,
    ).astype(BF16)
    small = jnp.pad(small, ((0, 0), (0, LANES - small.shape[1])))
    half_width = EXPERTS * sixth

    def for_core(at):
        return jnp.concatenate(
            [
                lax.dynamic_slice_in_dim(
                    master_key_value, side * QW + (2 * part + at) * half_width, half_width, 1
                )
                for side in range(2)
                for part in range(halves)
            ],
            axis=1,
        ).astype(BF16)

    kv_mine = jnp.concatenate([for_core(core), small], axis=1)
    kv_got = core_swap(jnp.concatenate([for_core(1 - core), small], axis=1))

    def block_for(rows, bits):
        other = expert_at ^ bits
        column = ((other % halves) * EXPERTS + other // halves) * sixth
        return jnp.concatenate(
            [
                lax.dynamic_slice_in_dim(rows, column, sixth, 1),
                lax.dynamic_slice_in_dim(rows, halves * half_width + column, sixth, 1),
                rows[:, 2 * halves * half_width :],
            ],
            axis=1,
        )

    kv_pair = in_core_order(core, kv_mine, kv_got, 0)
    kv_blocks = [block_for(kv_pair, bits) for bits in range(partners)]

    width_ff = master_gate_up.shape[2] // 2
    kv_blocks = [over_expert(block, bits) for bits, block in enumerate(kv_blocks)]
    kv_blocks, payload = together(kv_blocks, payload)
    token_blocks = [over_expert(payload, bits) for bits in range(partners)]
    arrived = jnp.zeros((2 * partners * local_rows, 2 * sixth + LANES), BF16)
    for block, at in zip(kv_blocks, places):
        arrived = lax.dynamic_update_slice_in_dim(arrived, block, at * 2 * local_rows, 0)
    arrived = arrived.reshape(partners, 2, local_rows, -1).transpose(1, 0, 2, 3)
    arrived = arrived.reshape(2 * partners * local_rows, -1)
    arrived, master_gate_up, _ = together(arrived, master_gate_up, attn_rows)
    gate_mine, gate_theirs = halves_of(core, master_gate_up[0])
    up_mine, up_theirs = halves_of(core, master_gate_up[1])
    gate_up_rows = fill(
        (2 * map_rows, 2 * width_ff),
        [
            (gate_mine.astype(BF16), row_mine, 0),
            (up_mine.astype(BF16), row_mine, width_ff),
            (core_swap(gate_theirs.astype(BF16)), row_got, 0),
            (core_swap(up_theirs.astype(BF16)), row_got, width_ff),
        ],
    )
    shared_whole = gather_split(chip, after(arrived, gate_up_rows, weight_attn))
    token_blocks, shared_whole = together(token_blocks, shared_whole)
    everyone = place_rows(token_blocks, places)
    kv_weight = shared_whole[:, : 2 * sixth]
    small_whole = shared_whole[:, 2 * sixth :]
    router_low = small_whole[:, : 2 * EXPERTS]
    router_f = router_low.astype(F32)
    gains_f = small_whole[:, 2 * EXPERTS : 2 * EXPERTS + 2].astype(F32).T
    total_count = jnp.sum(small_whole[:, 2 * EXPERTS + 2].astype(F32)) / local_rows

    weight_gate_up = gather_chips(gate_up_rows)
    down_mine, down_theirs = halves_of(core, master_down.astype(BF16).T)
    down_rows = fill(
        (2 * map_rows, width_ff),
        [(down_mine, row_mine, 0), (core_swap(down_theirs), row_got, 0)],
    )
    weight_down = gather_chips(down_rows)

    tables = rope_tables(token_count)
    inputs_all = everyone[:, :D].astype(F32)
    inverse_all = lax.rsqrt(jnp.mean(inputs_all * inputs_all, axis=-1, keepdims=True) + NORM_EPS)
    normed_all = (inputs_all * inverse_all * gains_f[0]).astype(BF16)
    inputs_f = tokens.astype(F32)
    inverse_one, normed_one = (
        lax.dynamic_slice_in_dim(table, expert_at * token_count, token_count, 0)
        for table in (inverse_all, normed_all)
    )
    marks_all = everyone[:, D:].astype(F32).reshape(sequences, token_count, LANES)
    named_all = jnp.any(marks_all[:, :, :TOP] == expert.astype(F32), axis=2)
    slot_all = slots_before(named_all[:, :, None])[:, :, 0]
    slots = jnp.arange(CAP, dtype=jnp.int32)
    pick_all = (named_all[:, None, :] & (slot_all[:, None, :] == slots[None, :, None])).astype(BF16)
    image_on = marks_all[:, :, TOP] > 0.0
    position = jnp.arange(token_count, dtype=jnp.int32)
    allowed = (position[:, None] >= position[None, :])[None] | (
        image_on[:, :, None] & image_on[:, None, :]
    )

    kv_heads = by_heads(matmul(normed_all, kv_weight), sequences)
    count = sixth // HD
    kv_own = jnp.concatenate(
        [rotate(kv_heads[:count], *tables).astype(BF16), kv_heads[count:].astype(BF16)]
    )
    query_pre = matmul(normed_all, weight_query)
    query_heads = rotate(by_heads(query_pre, sequences), *tables).astype(BF16)
    kv_shared = [over_expert(kv_own, step * halves) for step in range(EXPERTS - 1)]
    kv_shared.append(over_expert(after(kv_own, query_heads, down_rows), (EXPERTS - 1) * halves))

    def every_head(parts):
        whole = jnp.zeros((EXPERTS * count,) + parts[0].shape[1:], BF16)
        for step, part in enumerate(parts):
            whole = lax.dynamic_update_slice_in_dim(whole, part, (expert ^ step) * count, 0)
        return whole

    key_heads = every_head([part[:count] for part in kv_shared])
    value_heads = every_head([part[count:] for part in kv_shared])
    scores = heads_dot(query_heads, key_heads, 3, 3) * SCALE
    scores = jnp.where(allowed[None], scores, MASK_FILL)
    probs = jax.nn.softmax(scores, axis=-1)
    probs_low = probs.astype(BF16)
    attended_all = from_heads(heads_dot(probs_low, value_heads, 3, 2).astype(BF16))

    def per_sequence(table, rows, left_axis):
        blocks = rows.reshape(sequences, -1, rows.shape[1])
        picked = lax.dot_general(
            table, blocks, (((left_axis,), (1,)), ((0,), (0,))), preferred_element_type=F32
        )
        return picked.astype(BF16).reshape(-1, rows.shape[1])

    attended = per_sequence(pick_all, attended_all, 2)

    attn_pick, attn_back, attn_hit = route_tables(attn_routes, names)
    gates_attn = chosen_gates(matmul(normed_one, router_low[:, :EXPERTS]), attn_routes)
    branch_rows = jnp.concatenate(
        return_rows(matmul_back(attended, weight_project), partners, places)
    )
    branch = [matmul(attn_back[choice], branch_rows) for choice in range(TOP)]
    hidden = inputs_f + sum(gates_attn[:, choice, None] * branch[choice] for choice in range(TOP))

    inverse_two = lax.rsqrt(jnp.mean(hidden * hidden, axis=-1, keepdims=True) + NORM_EPS)
    normed_two = (hidden * inverse_two * gains_f[1]).astype(BF16)
    mlp_pick, mlp_back, mlp_hit = route_tables(mlp_routes, names)
    gates_mlp = chosen_gates(matmul(normed_two, router_low[:, EXPERTS:]), mlp_routes)
    placed = matmul(mlp_pick.reshape(-1, token_count), normed_two).astype(BF16)
    rows_two = send_rows(list(placed.reshape(partners, CAP, D)))
    gate_up_val = matmul(rows_two, weight_gate_up)
    gate_val, up_val = gate_up_val[:, :width_ff], gate_up_val[:, width_ff:]
    active = (jax.nn.silu(gate_val) * up_val).astype(BF16)
    mlp_rows = jnp.concatenate(return_rows(matmul_back(active, weight_down).astype(BF16), partners))
    mlp_branch = [matmul(mlp_back[choice], mlp_rows) for choice in range(TOP)]
    outputs = hidden + sum(gates_mlp[:, choice, None] * mlp_branch[choice] for choice in range(TOP))

    deviation = outputs - teacher.astype(F32)
    local_error = jnp.sum(valid_f[:, None] * deviation * deviation)
    grad_out = 2.0 * valid_f[:, None] * deviation / total_count

    def send_grads(pick, gates, hit, grad, where=None, by_block=False):
        gate_of = jnp.sum(gates[:, :, None] * hit, axis=1)
        rows = (gate_of.T[:, :, None] * grad[None]).astype(BF16)
        sent = jnp.einsum("kct,ktd->kcd", pick, rows, preferred_element_type=F32).astype(BF16)
        return send_rows(list(sent), where, by_block)

    rows_grad = send_grads(mlp_pick, gates_mlp, mlp_hit, grad_out, by_block=True)
    grad_down = matmul_rows(rows_grad, active).astype(BF16)
    grad_active = matmul(rows_grad, weight_down)
    sigmoid_gate = jax.nn.sigmoid(gate_val)
    grad_gate = (
        grad_active * up_val * sigmoid_gate * (1.0 + gate_val * (1.0 - sigmoid_gate))
    ).astype(BF16)
    grad_up = (grad_active * gate_val * sigmoid_gate).astype(BF16)
    grad_both = jnp.concatenate([grad_gate, grad_up], axis=1)
    down_sum = scatter_chips(grad_down)
    grad_gate_up = matmul_rows(rows_two, grad_both).astype(BF16)
    normed_two_rows = return_rows(
        matmul_back(after(grad_both, grad_down), weight_gate_up), partners
    )
    gate_up_sum = scatter_chips(after(grad_gate_up, down_sum, *normed_two_rows))
    grad_gates_mlp = jnp.stack(
        [jnp.sum(grad_out * mlp_branch[choice], axis=-1) for choice in range(TOP)], axis=1
    )
    grad_logits_mlp = gate_back(gates_mlp, grad_gates_mlp, mlp_routes)
    grad_normed_two = matmul(
        jnp.sum(mlp_back, axis=0), jnp.concatenate(normed_two_rows)
    ) + exact_back(grad_logits_mlp, router_f[:, EXPERTS:])
    grad_hidden_norm, grad_gain_two = norm_back(hidden, inverse_two, gains_f[1], grad_normed_two)
    grad_hidden = grad_out + grad_hidden_norm
    grad_router_two = exact_rows(normed_two.astype(F32), grad_logits_mlp)

    rows_grad_attn = send_grads(attn_pick, gates_attn, attn_hit, grad_hidden, places)
    grad_project = matmul_rows(rows_grad_attn, attended).astype(BF16)
    grad_attended = matmul(rows_grad_attn, weight_project).astype(BF16)
    grad_gates_attn = jnp.stack(
        [jnp.sum(grad_hidden * branch[choice], axis=-1) for choice in range(TOP)], axis=1
    )
    grad_logits_attn = gate_back(gates_attn, grad_gates_attn, attn_routes)
    grad_heads = by_heads(per_sequence(pick_all, grad_attended, 1), sequences)
    grad_probs = heads_dot(grad_heads, value_heads, 3, 3)
    inner = jnp.sum(probs * grad_probs, axis=-1, keepdims=True)
    grad_scores = (probs * (grad_probs - inner)).astype(BF16)
    grad_query_heads = heads_dot(grad_scores, key_heads, 3, 2) * SCALE
    grad_key_heads = heads_dot(grad_scores, query_heads, 2, 2) * SCALE
    grad_value_heads = heads_dot(probs_low, grad_heads, 2, 2)
    back_tables = (tables[0], -tables[1])
    grad_query_pre = from_heads(rotate(grad_query_heads, *back_tables).astype(BF16))
    grad_keys = rotate(grad_key_heads, *back_tables).astype(BF16)
    grad_values = grad_value_heads.astype(BF16)
    grad_query = matmul_rows(normed_all, grad_query_pre).astype(BF16)
    def heads_of(step):
        start = (expert ^ step) * count
        return jnp.concatenate(
            [
                lax.dynamic_slice_in_dim(table, start, count, 0)
                for table in (grad_keys, grad_values)
            ]
        )

    grad_kv_parts = [heads_of(step) for step in range(EXPERTS)]
    total_error = all_sum(after(local_error, grad_query).reshape(1, 1))[0, 0]
    grad_kv_parts[-1] = after(grad_kv_parts[-1], grad_query, total_error)
    grad_kv = sum(
        over_expert(part, step * halves).astype(F32) for step, part in enumerate(grad_kv_parts)
    ).astype(BF16)
    grad_kv = from_heads(grad_kv)
    grad_kv_weight = matmul_rows(normed_all, grad_kv).astype(BF16)
    normed_one_partial = matmul_back(grad_query_pre, weight_query) + matmul_back(
        grad_kv, kv_weight
    )
    grad_normed_router = exact_back(grad_logits_attn, router_f[:, :EXPERTS])
    grad_gain_one = jnp.sum(normed_one_partial * inputs_all * inverse_all, axis=0) + jnp.sum(
        grad_normed_router * inputs_f * inverse_one, axis=0
    )
    grad_small = jnp.concatenate(
        [
            exact_rows(normed_one.astype(F32), grad_logits_attn),
            grad_router_two,
            grad_gain_one[:, None],
            grad_gain_two[:, None],
        ],
        axis=1,
    ).astype(BF16)
    grad_small = jnp.pad(grad_small, ((0, 0), (0, LANES - grad_small.shape[1])))
    last_rows = fill(
        (grad_query.shape[0], 2 * width_attn + 2 * sixth + LANES),
        [
            (grad_project, 0, width_attn),
            (grad_query, 0, 0),
            (grad_kv_weight, 0, 2 * width_attn),
            (grad_small, 0, 2 * width_attn + 2 * sixth),
        ],
    )
    last_sum = scatter_chips(after(last_rows, gate_up_sum))
    gate_up_mine, gate_up_other = exchange_rows(core, gate_up_sum)
    reduced_gate_up = jnp.stack(
        [
            in_core_order(
                core,
                gate_up_mine[:, at * width_ff : (at + 1) * width_ff],
                gate_up_other[:, at * width_ff : (at + 1) * width_ff],
                1,
            )
            for at in range(2)
        ]
    )
    reduced_gate_up = with_layout_constraint(
        reduced_gate_up, Layout(major_to_minor=(0, 1, 2))
    ).astype(F32)
    update_gate_up = adam_step(moment_gate_up, square_gate_up, reduced_gate_up)
    normed_one_rows = return_rows(
        after(normed_one_partial, last_rows), partners, places, update_gate_up
    )
    grad_normed_one = sum(rows.astype(F32) for rows in normed_one_rows) + grad_normed_router
    grad_inputs_norm, _ = norm_back(inputs_f, inverse_one, gains_f[0], grad_normed_one)
    input_grad = grad_hidden + grad_inputs_norm

    down_sum, _ = together(down_sum, normed_one_rows)
    down_mine, down_other = exchange_rows(core, down_sum)
    reduced_down = turned(in_core_order(core, down_mine, down_other, 1))
    update_down = adam_step(moment_down, square_down, reduced_down)

    last_mine, last_other = exchange_rows(core, after(last_sum, *update_down))
    attn_mine, attn_other = last_mine[:, : 2 * width_attn], last_other[:, : 2 * width_attn]
    shared_mine, shared_theirs = [
        rows[:, 2 * width_attn :].reshape(partners, local_rows, -1)
        for rows in (last_mine, last_other)
    ]
    shared_pair = jnp.where(
        core == 0, jnp.stack([shared_mine, shared_theirs]), jnp.stack([shared_theirs, shared_mine])
    )
    received = jnp.stack(
        [
            over_expert(lax.dynamic_index_in_dim(shared_pair, expert_at ^ bits, 1, keepdims=False), bits)
            for bits in range(partners)
        ]
    )
    query_mine, project_mine = attn_mine[:, :width_attn], attn_mine[:, width_attn:]
    query_other, project_other = attn_other[:, :width_attn], attn_other[:, width_attn:]
    small_sum = jnp.sum(received[..., -LANES:].astype(F32), axis=(0, 1))
    received = jnp.stack(
        [lax.dynamic_index_in_dim(received, expert_at ^ at, 0, keepdims=False) for at in range(partners)]
    )
    reduced_kv = (
        received[..., :-LANES]
        .reshape(EXPERTS, halves, 2, local_rows, 2, sixth)
        .transpose(3, 4, 1, 2, 0, 5)
        .reshape(local_rows, -1)
        .astype(F32)
    )
    reduced_router = small_sum[:, : 2 * EXPERTS]
    reduced_gains = small_sum[:, 2 * EXPERTS : 2 * EXPERTS + 2].T
    reduced_query = with_layout_constraint(
        in_core_order(core, query_mine, query_other, 1), Layout(major_to_minor=(0, 1))
    ).astype(F32)
    reduced_project = turned(in_core_order(core, project_mine, project_other, 1))
    loss_value = total_error / total_count
    return (
        outputs,
        loss_value,
        input_grad,
        *adam_step(moment_query, square_query, reduced_query),
        *adam_step(moment_project, square_project, reduced_project),
        *update_gate_up,
        *update_down,
        *adam_step(moment_key_value, square_key_value, reduced_kv),
        *adam_step(moment_router, square_router, reduced_router),
        *adam_step(moment_gains, square_gains, reduced_gains),
    )


def solution(mesh):
    rows = P(("dp", "expert"), None)
    flat = P(("dp", "expert"))
    columns = P(None, ("dp", "expert"))
    query, project, gate_up = P("dp", "expert"), P("expert", "dp"), P(None, "dp", "expert")
    weights = (query, project, gate_up, project, rows, rows, columns)
    return jax.shard_map(
        body,
        mesh=mesh,
        in_specs=(rows, rows, rows, rows, flat, flat)
        + tuple(spec for spec in weights for _ in range(3)),
        out_specs=(rows, P(), rows) + tuple(spec for spec in weights for _ in range(4)),
        check_vma=False,
    )
```
